32 devices in a mesh: dom: 8 (over y, x, core), grp: 4 (over z).
Axes of the slice: x: 2, y: 2, z: 4, core: 2. Of those that a mesh axis runs over, the one named last changes fastest.
Arguments:
- valence: float32 [64, 64, 512], P('dom', None, 'grp')
- start_potential: float32 [64, 64, 512], P('dom', None, 'grp'), may hold values from -3 to 3
- atom_tiles: float32 [8192, 512], P(('dom', 'grp')), may hold values from -12 to 12
- atom_home: int32 [8192, 1], P(('dom', 'grp')), may hold values from 0 to 31; in each aligned block of 256 rows (0 to 255, 256 to 511, ...) at most 16 rows name the same one
- atom_offset_x: int32 [8192, 1], P(('dom', 'grp')), may hold values from 0 to 7
- atom_offset_y: int32 [8192, 1], P(('dom', 'grp')), may hold values from 0 to 63
- atom_offset_z: int32 [8192, 1], P(('dom', 'grp')), may hold values from 0 to 120
- atom_size: int32 [8192, 1], P(('dom', 'grp')), may hold values from 4 to 8
Outputs:
- potential: float32 [64, 64, 512], P('dom', None, 'grp')
- stress: float32 [6], replicated
The draws below stay inside these ranges and needn't reach their ends.
Inputs may be any that keep to these rules, and one draw needn't show every extreme that they name: `atom_home`: at most 16 atoms among the rows of one device share a home, and some home has exactly 16 of them.
All inputs are finite; a program needn't handle non-finite values.
Results may differ from the reference program's by a relative error of at most 0.00014.
Values sent between devices are 32-bit elements; how exact they have to be, the bound alone decides.
A program may use at most 128 MiB of HBM per device.

```python
import math
import jax
import jax.numpy as jnp
import numpy as np
from jax import lax

CX = 8
CY = 64
CZ = 128
ATOMS_DEV = 256
TE = 8
NU = 2
TE3 = 512
CAP = 16
ATOMS = 8192
NX = 64
NZ = 512
N_GRP = 4
DEVICES = 32


def draw_valence(key, part):
    position_x = jnp.arange(NX, dtype=jnp.float32) / NX
    growth = (1.0 + 2.0 * position_x)[:, None, None]
    rough_part = jnp.clip(jax.random.normal(key, (NX, CY, NZ), jnp.float32), -5.0, 5.0)
    return rough_part * growth


def set_ends(values, rng, least, high):
    extent = values.shape
    place = [jax.random.randint(jax.random.fold_in(rng, axis), (), 0, extent[axis]) for axis in range(len(extent))]
    values = values.at[tuple(place)].set(least)
    longest = extent.index(max(extent))
    place[longest] = (place[longest] + 1) % extent[longest]
    return values.at[tuple(place)].set(high)


def shard_levels(key, dims, pieces, smallest, top_value):
    def one(axis_at, parts):
        steps = jax.random.uniform(jax.random.fold_in(jax.random.fold_in(key, 6), axis_at), (parts,), jnp.float32, smallest / len(pieces), top_value / len(pieces))
        return jnp.repeat(jnp.exp(steps), dims[axis_at] // parts).reshape((-1,) + (1,) * (len(dims) - axis_at - 1))

    factor_of = one(*pieces[0])
    for cut in pieces[1:]:
        factor_of = factor_of * one(*cut)
    return factor_of


def routed_block(rng, own, number, rows, number_of, top, most, skew):
    sequence = jax.random.permutation(rng, number_of)
    crowded, usual = shares(number_of, rows * top, most, skew, True), shares(number_of, rows * top, most, skew, False)
    places = jnp.arange(number_of)

    def named(lengths, offset_by):
        used = int((lengths > 0).sum())
        fixed = max(1, used // 4)
        passed = fixed + (places - fixed + offset_by * (used - fixed)) % max(1, number_of - fixed)
        return jnp.zeros((number_of,), jnp.int32).at[sequence[jnp.where(places < fixed, places, passed)]].set(jnp.asarray(lengths, jnp.int32))

    lengths = jnp.where(number % 4 == 0, named(crowded, number // 4), named(usual, number - number // 4 - 1))
    mixed = jax.random.permutation(jax.random.fold_in(own, 3), number_of)
    donor, receiver = mixed[0:number_of // 2 * 2:2], mixed[1:number_of // 2 * 2:2]
    room = jnp.minimum(lengths[donor] - 1, most - lengths[receiver]) // 2
    room = jnp.where((donor == sequence[0]) | (receiver == sequence[0]) | (lengths[receiver] == 0), 0, jnp.maximum(room, 0))
    passed = jax.random.randint(jax.random.fold_in(own, 4), (number_of // 2,), 0, 1 << 20) % (room + 1)
    lengths = lengths.at[donor].add(-passed).at[receiver].add(passed)
    items = jnp.searchsorted(jnp.cumsum(lengths), jnp.arange(rows * top), side="right").astype(jnp.int32)
    table = items.reshape(top, rows).T
    table = table[jax.random.permutation(jax.random.fold_in(own, 1), rows)]
    offset_by = jax.random.randint(jax.random.fold_in(own, 2), (rows, 1), 0, top)
    return jnp.take_along_axis(table, (jnp.arange(top)[None, :] + offset_by) % top, axis=1)


def shares(count, total, most, slope, full):
    loads = [(1 << 20) // math.isqrt(rank ** slope) + 1 for rank in range(1, count + 1)]
    largest = most if full else min(most, max(-(-total // count), total * loads[0] // sum(loads)))
    least = 1 if total - largest >= count - 1 else 0
    counts, surplus = [largest] + [least] * (count - 1), total - largest - least * (count - 1)
    while surplus > 0:
        candidates = [i for i in range(1, count) if counts[i] < largest] or [i for i in range(1, count) if counts[i] < most]
        mass, budget = sum([loads[i] for i in candidates]), surplus
        for i in candidates:
            extra = min(most - counts[i], max(1, budget * loads[i] // mass), surplus)
            counts[i] = counts[i] + extra
            surplus = surplus - extra
    return np.array(counts)


def scatter_about(own_key, extent, scale, bound, cuts=(), kind=jnp.bfloat16):
    drawn = jax.random.normal(own_key, extent, jnp.float32) * scale
    if len(cuts) > 0:
        drawn = shard_levels(own_key, extent, cuts, -0.22, 0.18) * drawn
    return jnp.clip(drawn, min=-bound, max=bound).astype(kind)


def setup_inputs(seed: int = 0) -> dict:
    arg_keys = jax.random.split(jax.random.key(seed), 9)
    valence = draw_valence(jax.random.fold_in(arg_keys[8], 71), 0)
    start_potential = scatter_about(arg_keys[1], (NX, CY, NZ), 0.5, 3.0, ((0, 8), (2, 4)), jnp.float32)
    atom_tiles = scatter_about(arg_keys[2], (ATOMS, TE3), 2.0, 12.0, ((0, 32),), jnp.float32)
    atom_home_keys = jax.random.split(jax.random.fold_in(arg_keys[3], 1), ATOMS // ATOMS_DEV)
    atom_home_turns = jax.random.permutation(jax.random.fold_in(arg_keys[3], 3), ATOMS // ATOMS_DEV)
    atom_home = jax.vmap(lambda own, number: routed_block(jax.random.fold_in(arg_keys[3], 2), own, number, ATOMS_DEV, DEVICES, 1, CAP, 2))(atom_home_keys, atom_home_turns).reshape((ATOMS, 1))
    atom_offset_x = set_ends(jax.random.randint(arg_keys[4], (ATOMS, 1), 0, CX), jax.random.fold_in(arg_keys[4], 1), 0, CX - 1).astype(jnp.int32)
    atom_offset_y = set_ends(jax.random.randint(arg_keys[5], (ATOMS, 1), 0, CY), jax.random.fold_in(arg_keys[5], 1), 0, CY - 1).astype(jnp.int32)
    atom_offset_z = set_ends(jax.random.randint(arg_keys[6], (ATOMS, 1), 0, CZ - TE + 1), jax.random.fold_in(arg_keys[6], 1), 0, CZ - TE).astype(jnp.int32)
    atom_size = set_ends(jax.random.randint(arg_keys[7], (ATOMS, 1), TE // 2, TE + 1), jax.random.fold_in(arg_keys[7], 1), TE // 2, TE).astype(jnp.int32)
    return {"valence": valence, "start_potential": start_potential, "atom_tiles": atom_tiles, "atom_home": atom_home, "atom_offset_x": atom_offset_x, "atom_offset_y": atom_offset_y, "atom_offset_z": atom_offset_z, "atom_size": atom_size}


DAMPING = 2.0 / 3.0

def sine_basis(length_now):
    steps_now = jnp.arange(length_now, dtype=jnp.float32)
    table = jnp.sqrt(2.0 / (length_now + 1)) * jnp.sin(jnp.pi * (steps_now[:, None] + 1.0) * (steps_now[None, :] + 1.0) / (length_now + 1))
    values = 2.0 - 2.0 * jnp.cos(jnp.pi * (steps_now + 1.0) / (length_now + 1))
    return (table, values)

def cyclic_basis(length_now):
    steps_now = jnp.arange(length_now, dtype=jnp.float32)[:, None]
    column = jnp.arange(length_now, dtype=jnp.int32)[None, :]
    freqs = ((column + 1) // 2).astype(jnp.float32)
    angles = 2.0 * jnp.pi * freqs * steps_now / length_now
    use_sine = (column % 2 == 0) & (column > 0)
    edge_cols = (column == 0) | (column == length_now - 1)
    scales = jnp.where(edge_cols, jnp.sqrt(1.0 / length_now), jnp.sqrt(2.0 / length_now))
    table = scales * jnp.where(use_sine, jnp.sin(angles), jnp.cos(angles))
    values = 2.0 - 2.0 * jnp.cos(2.0 * jnp.pi * freqs[0] / length_now)
    return (table, values)

def exact_solve(source, spacing_sq):
    table_x, values_x = sine_basis(source.shape[0])
    table_y, values_y = cyclic_basis(source.shape[1])
    table_z, values_z = sine_basis(source.shape[2])
    highest = lax.Precision.HIGHEST
    modes = jnp.einsum('ia,ijk->ajk', table_x, source, precision=highest)
    modes = jnp.einsum('jb,ajk->abk', table_y, modes, precision=highest)
    modes = jnp.einsum('kc,abk->abc', table_z, modes, precision=highest)
    modes = modes * spacing_sq / (values_x[:, None, None] + values_y[None, :, None] + values_z[None, None, :])
    result = jnp.einsum('kc,abc->abk', table_z, modes, precision=highest)
    result = jnp.einsum('jb,abk->ajk', table_y, result, precision=highest)
    return jnp.einsum('ia,ajk->ijk', table_x, result, precision=highest)

def operate(current, spacing_sq):
    padded = jnp.pad(current, ((1, 1), (0, 0), (1, 1)))
    beside = padded[2:, :, 1:-1] + padded[:-2, :, 1:-1]
    beside = beside + jnp.roll(current, 1, axis=1) + jnp.roll(current, -1, axis=1)
    beside = beside + padded[1:-1, :, 2:] + padded[1:-1, :, :-2]
    return (6.0 * current - beside) / spacing_sq

def smooth(current, source, spacing_sq, sweeps):
    for step_index in range(sweeps):
        if current is None:
            current = DAMPING * spacing_sq / 6.0 * source
        else:
            current = current + DAMPING * spacing_sq / 6.0 * (source - operate(current, spacing_sq))
    return current

def restrict(residue):
    dims_now = residue.shape
    coarse = residue.reshape(dims_now[0] // 2, 2, dims_now[1] // 2, 2, dims_now[2] // 2, 2)
    return coarse.mean(axis=(1, 3, 5))

def prolong(correction):
    dims_now = correction.shape
    spread = jnp.broadcast_to(correction[:, None, :, None, :, None], (dims_now[0], 2, dims_now[1], 2, dims_now[2], 2))
    return spread.reshape(dims_now[0] * 2, dims_now[1] * 2, dims_now[2] * 2)

def vcycle(level_index, current, source):
    spacing_sq = 4.0 ** level_index
    if level_index == 3:
        return exact_solve(source, spacing_sq)
    current = smooth(current, source, spacing_sq, NU)
    residue = source - operate(current, spacing_sq)
    correction = vcycle(level_index + 1, None, restrict(residue))
    current = current + prolong(correction)
    return smooth(current, source, spacing_sq, NU)

def reference(valence, start_potential, atom_tiles, atom_home, atom_offset_x, atom_offset_y, atom_offset_z, atom_size):
    tile_index = jnp.arange(TE, dtype=jnp.int32)
    inside = tile_index[None, :] < atom_size
    inside_cube = inside[:, :, None, None] & inside[:, None, :, None] & inside[:, None, None, :]
    masked = atom_tiles * inside_cube.reshape(atom_tiles.shape).astype(jnp.float32)
    home_device = atom_home[:, 0]
    corner_x = home_device // N_GRP * CX + atom_offset_x[:, 0]
    corner_z = home_device % N_GRP * CZ + atom_offset_z[:, 0]
    cells_x = corner_x[:, None] + tile_index[None, :]
    cells_y = (atom_offset_y[:, 0][:, None] + tile_index[None, :]) % CY
    cells_z = corner_z[:, None] + tile_index[None, :]
    atom_count = atom_tiles.shape[0]
    tile_shape = (atom_count, TE, TE, TE)
    index_x = jnp.broadcast_to(cells_x[:, :, None, None], tile_shape)
    index_y = jnp.broadcast_to(cells_y[:, None, :, None], tile_shape)
    index_z = jnp.broadcast_to(cells_z[:, None, None, :], tile_shape)
    compensation = jnp.zeros(valence.shape, jnp.float32).at[index_x, index_y, index_z].add(masked.reshape(tile_shape), mode='drop')
    density = valence + compensation
    potential = vcycle(0, start_potential, density)
    padded = jnp.pad(potential, ((1, 1), (0, 0), (1, 1)))
    grad_x = 0.5 * (padded[2:, :, 1:-1] - padded[:-2, :, 1:-1])
    grad_y = 0.5 * (jnp.roll(potential, -1, axis=1) - jnp.roll(potential, 1, axis=1))
    grad_z = 0.5 * (padded[1:-1, :, 2:] - padded[1:-1, :, :-2])
    totals = jnp.stack([jnp.sum(grad_x * grad_x), jnp.sum(grad_y * grad_y), jnp.sum(grad_z * grad_z), jnp.sum(grad_y * grad_z), jnp.sum(grad_x * grad_z), jnp.sum(grad_x * grad_y), jnp.sum(potential * density)])
    cell_count = potential.shape[0] * potential.shape[1] * potential.shape[2]
    products = totals[:6] / cell_count
    energy = 0.5 * totals[6] / cell_count
    diagonal_mask = jnp.array([1.0, 1.0, 1.0, 0.0, 0.0, 0.0], jnp.float32)
    stress = products - energy * diagonal_mask
    return (potential, stress)
```

```python
import jax
import jax.numpy as jnp
from jax import lax
from jax.experimental import pallas as pl
from jax.experimental.pallas import tpu as pltpu
from jax.sharding import PartitionSpec as P
import functools

TE = 8
NU = 2


DAMPING = 2.0 / 3.0


def extended(value, sides, width):
    for axis, dim in sides:
        peers, length = (lax.axis_size(axis), value.shape[dim])
        up = [(i, (i + 1) % peers) for i in range(peers - 1)]
        down = [(j, i) for i, j in up]
        last = lax.slice_in_dim(value, length - width, length, axis=dim)
        leading = lax.slice_in_dim(value, 0, width, axis=dim)
        before = lax.ppermute(last, axis, up)
        after = lax.ppermute(leading, axis, down)
        value = jnp.concatenate([before, value, after], axis=dim)
    return value


def from_behind(block, axis, distance):
    devices = range(lax.axis_size(axis))
    route = [(i - distance, i) for i in devices if i - distance in devices]
    return lax.ppermute(block, axis, route)


def sine_basis(length_now):
    steps_now = jnp.arange(length_now, dtype=jnp.float32)
    table = jnp.sqrt(2.0 / (length_now + 1)) * jnp.sin(
        jnp.pi * (steps_now[:, None] + 1.0) * (steps_now[None, :] + 1.0) / (length_now + 1)
    )
    values = 2.0 - 2.0 * jnp.cos(jnp.pi * (steps_now + 1.0) / (length_now + 1))
    return (table, values)


def cyclic_basis(length_now):
    steps_now = jnp.arange(length_now, dtype=jnp.float32)[:, None]
    column = jnp.arange(length_now, dtype=jnp.int32)[None, :]
    freqs = ((column + 1) // 2).astype(jnp.float32)
    angles = 2.0 * jnp.pi * freqs * steps_now / length_now
    use_sine = (column % 2 == 0) & (column > 0)
    edge_cols = (column == 0) | (column == length_now - 1)
    scales = jnp.where(edge_cols, jnp.sqrt(1.0 / length_now), jnp.sqrt(2.0 / length_now))
    table = scales * jnp.where(use_sine, jnp.sin(angles), jnp.cos(angles))
    values = 2.0 - 2.0 * jnp.cos(2.0 * jnp.pi * freqs[0] / length_now)
    return (table, values)


def exact_solve(source, spacing_sq):
    table_x, values_x = sine_basis(source.shape[0])
    table_y, values_y = cyclic_basis(source.shape[1])
    table_z, values_z = sine_basis(source.shape[2])
    highest = lax.Precision.HIGHEST
    modes = jnp.einsum("ia,ijk->ajk", table_x, source, precision=highest)
    modes = jnp.einsum("jb,ajk->abk", table_y, modes, precision=highest)
    modes = jnp.einsum("kc,abk->abc", table_z, modes, precision=highest)
    modes = (
        modes
        * spacing_sq
        / (values_x[:, None, None] + values_y[None, :, None] + values_z[None, None, :])
    )
    result = jnp.einsum("kc,abc->abk", table_z, modes, precision=highest)
    result = jnp.einsum("jb,abk->ajk", table_y, result, precision=highest)
    return jnp.einsum("ia,ajk->ijk", table_x, result, precision=highest)


def neighbours(current, layout):
    if layout == "split":
        return extended(current, (("dom", 0), ("grp", 2)), 1)
    return jnp.pad(current, ((1, 1), (0, 0), (1, 1)))


def operate(current, spacing_sq, layout):
    padded = neighbours(current, layout)
    beside = padded[2:, :, 1:-1] + padded[:-2, :, 1:-1]
    beside = beside + jnp.roll(current, 1, axis=1) + jnp.roll(current, -1, axis=1)
    beside = beside + padded[1:-1, :, 2:] + padded[1:-1, :, :-2]
    return (6.0 * current - beside) / spacing_sq


def smooth(current, source, spacing_sq, sweeps, layout):
    for step_index in range(sweeps):
        if current is None:
            current = DAMPING * spacing_sq / 6.0 * source
        else:
            current = current + DAMPING * spacing_sq / 6.0 * (
                source - operate(current, spacing_sq, layout)
            )
    return current


def restrict(residue):
    dims_now = residue.shape
    coarse = residue.reshape(dims_now[0] // 2, 2, dims_now[1] // 2, 2, dims_now[2] // 2, 2)
    return coarse.mean(axis=(1, 3, 5))


def prolong(correction):
    dims_now = correction.shape
    spread = jnp.broadcast_to(
        correction[:, None, :, None, :, None], (dims_now[0], 2, dims_now[1], 2, dims_now[2], 2)
    )
    return spread.reshape(dims_now[0] * 2, dims_now[1] * 2, dims_now[2] * 2)


def vcycle(level_index, current, source, layout, gather_level):
    if layout == "split" and level_index == gather_level:
        column = lax.all_gather(source, "grp", axis=2, tiled=True)
        whole_grid = lax.all_gather(column, "dom", axis=0, tiled=True)
        joined = vcycle(level_index, None, whole_grid, "whole", gather_level)
        own_width = source.shape[0]
        own_depth = source.shape[2]
        mine = lax.dynamic_slice_in_dim(joined, lax.axis_index("dom") * own_width, own_width, 0)
        return lax.dynamic_slice_in_dim(mine, lax.axis_index("grp") * own_depth, own_depth, 2)
    spacing_sq = 4.0**level_index
    if level_index == 3:
        return exact_solve(source, spacing_sq)
    current = smooth(current, source, spacing_sq, NU, layout)
    residue = source - operate(current, spacing_sq, layout)
    correction = vcycle(level_index + 1, None, restrict(residue), layout, gather_level)
    current = current + prolong(correction)
    return smooth(current, source, spacing_sq, NU, layout)


ACCS = 4
OFFSET_ROWS = 8


def deposit_kernel(capacity, offsets_ref, tiles_ref, out_ref, *grids):
    slots = offsets_ref.shape[0] // 3
    width_y = out_ref.shape[1]
    lane = lax.broadcasted_iota(jnp.int32, (TE, 128), 1)
    low, high = (lane // TE == TE - 1, lane // TE == 2 * TE - 1)
    for grid in grids:
        grid[...] = jnp.zeros_like(grid)

    def step(i, carry):
        for j, grid in enumerate(grids):
            slot = i * len(grids) + j
            device = slot // capacity
            first = (slot % capacity) * 4
            at_x = offsets_ref[slot]
            at_y = width_y - offsets_ref[slots + slot]
            at_z = offsets_ref[2 * slots + slot]
            parts = []
            for q in range(4):
                line = tiles_ref[device, pl.ds(first + q, 1), :]
                line = jnp.broadcast_to(line, (TE, 128))
                line = pltpu.roll(line, 0, 1, stride=TE, stride_axis=0)
                for mask, shift in ((low, (at_z + 72) % 128), (high, (at_z + 8) % 128)):
                    kept = jnp.where(mask, line, 0.0)
                    parts.append(pltpu.roll(kept, shift, 1))
            for a, part in enumerate(parts):
                spot = (at_x + a, pl.ds(at_y, TE), slice(None))
                grid[spot] = grid[spot] + part
        return carry

    lax.fori_loop(0, slots // len(grids), step, 0)
    total = grids[0][...]
    for grid in grids[1:]:
        total = total + grid[...]
    rows = width_y + TE
    held = lax.broadcasted_iota(jnp.int32, (width_y, rows), 1)
    wanted = lax.broadcasted_iota(jnp.int32, (width_y, rows), 0)
    fold = ((rows - 1 - held) % width_y == wanted).astype(jnp.float32)
    for x in range(out_ref.shape[0]):
        out_ref[x] = jnp.dot(
            fold, total[x], precision=lax.Precision.HIGHEST, preferred_element_type=jnp.float32
        )


def deposit(tiles, offsets, capacity, extent):
    width_x, width_y, width_z = extent
    vmem = pl.BlockSpec(memory_space=pltpu.VMEM)
    return pl.pallas_call(
        functools.partial(deposit_kernel, capacity),
        out_shape=jax.ShapeDtypeStruct((width_x + TE, width_y, width_z), jnp.float32),
        in_specs=[pl.BlockSpec(memory_space=pltpu.SMEM), vmem],
        out_specs=vmem,
        scratch_shapes=[pltpu.VMEM((width_x + TE, width_y + TE, width_z), jnp.float32)] * ACCS,
        compiler_params=pltpu.CompilerParams(vmem_limit_bytes=32 * 1024 * 1024),
        name="deposit",
    )(offsets, tiles)


def shards(
    valence,
    start_potential,
    atom_tiles,
    atom_home,
    atom_offset_x,
    atom_offset_y,
    atom_offset_z,
    atom_size,
):
    domain_count = lax.axis_size("dom")
    group_count = lax.axis_size("grp")
    device_count = domain_count * group_count
    atoms_here = atom_tiles.shape[0]
    tile_cells = atom_tiles.shape[1]
    capacity = 2 * atoms_here // device_count
    tile_index = jnp.arange(TE, dtype=jnp.int32)
    inside = tile_index[None, :] < atom_size
    inside_cube = inside[:, :, None, None] & inside[:, None, :, None] & inside[:, None, None, :]
    masked = atom_tiles * inside_cube.reshape(atom_tiles.shape).astype(jnp.float32)
    targets = jnp.arange(device_count, dtype=jnp.int32)
    matches = (atom_home == targets[None, :]).astype(jnp.int32)
    before = jnp.cumsum(matches, axis=0) - matches
    slot_rank = jnp.sum(before * matches, axis=1)
    slot_index = atom_home[:, 0] * capacity + slot_rank
    offsets = jnp.concatenate([atom_offset_x, atom_offset_y, atom_offset_z], axis=1)
    slots = device_count * capacity
    send_tiles = jnp.zeros((slots, tile_cells), jnp.float32).at[slot_index].set(masked)
    send_offsets = jnp.zeros((slots, 3), jnp.float32).at[slot_index].set(offsets.astype(jnp.float32))
    send_offsets = send_offsets.reshape(device_count, capacity, 3).transpose(0, 2, 1)
    send_offsets = jnp.pad(send_offsets, ((0, 0), (0, OFFSET_ROWS - 3), (0, 128 - capacity)))
    tile_rows = capacity * tile_cells // 128
    send = jnp.concatenate([send_tiles.reshape(device_count, tile_rows, 128), send_offsets], axis=1)
    got = lax.all_to_all(send, ("dom", "grp"), split_axis=0, concat_axis=0, tiled=True)
    got_offsets = got[:, tile_rows : tile_rows + 3, :capacity].transpose(1, 0, 2)
    got_offsets = got_offsets.reshape(-1).astype(jnp.int32)
    width_x, width_y, width_z = valence.shape
    deposit_grid = deposit(got, got_offsets, capacity, valence.shape)
    spill_planes = deposit_grid[width_x:]
    incoming = from_behind(spill_planes, "dom", 1)
    local_grid = deposit_grid[:width_x].at[:TE].add(incoming)
    density = valence + local_grid
    gather_level = 2
    potential = vcycle(0, start_potential, density, "split", gather_level)
    padded = neighbours(potential, "split")
    grad_x = 0.5 * (padded[2:, :, 1:-1] - padded[:-2, :, 1:-1])
    grad_y = 0.5 * (jnp.roll(potential, -1, axis=1) - jnp.roll(potential, 1, axis=1))
    grad_z = 0.5 * (padded[1:-1, :, 2:] - padded[1:-1, :, :-2])
    local_totals = jnp.stack(
        [
            jnp.sum(grad_x * grad_x),
            jnp.sum(grad_y * grad_y),
            jnp.sum(grad_z * grad_z),
            jnp.sum(grad_y * grad_z),
            jnp.sum(grad_x * grad_z),
            jnp.sum(grad_x * grad_y),
            jnp.sum(potential * density),
        ]
    )
    totals = lax.psum(local_totals, ("dom", "grp"))
    cell_count = width_x * width_y * width_z * device_count
    products = totals[:6] / cell_count
    energy = 0.5 * totals[6] / cell_count
    diagonal_mask = jnp.array([1.0, 1.0, 1.0, 0.0, 0.0, 0.0], jnp.float32)
    stress = products - energy * diagonal_mask
    return (potential, stress)


def solution(mesh):
    in_specs = (
        P("dom", None, "grp"),
        P("dom", None, "grp"),
        P(("dom", "grp"), None),
        P(("dom", "grp"), None),
        P(("dom", "grp"), None),
        P(("dom", "grp"), None),
        P(("dom", "grp"), None),
        P(("dom", "grp"), None),
    )
    out_specs = (P("dom", None, "grp"), P())
    return jax.shard_map(shards, mesh=mesh, in_specs=in_specs, out_specs=out_specs, check_vma=False)
```

```python
import jax
import jax.numpy as jnp
from jax import lax
from jax.experimental import pallas as pl
from jax.experimental.pallas import tpu as pltpu
from jax.sharding import PartitionSpec as P
import functools
import numpy as np

TE = 8
HALO = 3
HIGHEST = lax.Precision.HIGHEST


ACCS = 4
OFFSET_ROWS = 8


def deposit_kernel(capacity, offsets_ref, tiles_ref, out_ref, *grids):
    slots = offsets_ref.shape[0] // 3
    width_y = out_ref.shape[1]
    lane = lax.broadcasted_iota(jnp.int32, (TE, 128), 1)
    low, high = (lane // TE == TE - 1, lane // TE == 2 * TE - 1)
    for grid in grids:
        grid[...] = jnp.zeros_like(grid)

    def step(i, carry):
        for j, grid in enumerate(grids):
            slot = i * len(grids) + j
            device = slot // capacity
            first = (slot % capacity) * 4
            at_x = offsets_ref[slot]
            at_y = width_y - offsets_ref[slots + slot]
            at_z = offsets_ref[2 * slots + slot]
            parts = []
            for q in range(4):
                line = tiles_ref[device, pl.ds(first + q, 1), :]
                line = jnp.broadcast_to(line, (TE, 128))
                line = pltpu.roll(line, 0, 1, stride=TE, stride_axis=0)
                for mask, shift in ((low, (at_z + 72) % 128), (high, (at_z + 8) % 128)):
                    kept = jnp.where(mask, line, 0.0)
                    parts.append(pltpu.roll(kept, shift, 1))
            for a, part in enumerate(parts):
                spot = (at_x + a, pl.ds(at_y, TE), slice(None))
                grid[spot] = grid[spot] + part
        return carry

    lax.fori_loop(0, slots // len(grids), step, 0)
    total = grids[0][...]
    for grid in grids[1:]:
        total = total + grid[...]
    rows = width_y + TE
    held = lax.broadcasted_iota(jnp.int32, (width_y, rows), 1)
    wanted = lax.broadcasted_iota(jnp.int32, (width_y, rows), 0)
    fold = ((rows - 1 - held) % width_y == wanted).astype(jnp.float32)
    for x in range(out_ref.shape[0]):
        out_ref[x] = jnp.dot(
            fold, total[x], precision=lax.Precision.HIGHEST, preferred_element_type=jnp.float32
        )


def deposit(tiles, offsets, capacity, extent):
    width_x, width_y, width_z = extent
    vmem = pl.BlockSpec(memory_space=pltpu.VMEM)
    return pl.pallas_call(
        functools.partial(deposit_kernel, capacity),
        out_shape=jax.ShapeDtypeStruct((width_x + TE, width_y, width_z), jnp.float32),
        in_specs=[pl.BlockSpec(memory_space=pltpu.SMEM), vmem],
        out_specs=vmem,
        scratch_shapes=[pltpu.VMEM((width_x + TE, width_y + TE, width_z), jnp.float32)] * ACCS,
        compiler_params=pltpu.CompilerParams(vmem_limit_bytes=32 * 1024 * 1024),
        name="deposit",
    )(offsets, tiles)


def sine_table(length):
    steps = np.arange(length) + 1.0
    table = np.sqrt(2.0 / (length + 1)) * np.sin(np.pi * np.outer(steps, steps) / (length + 1))
    return table, 2.0 - 2.0 * np.cos(np.pi * steps / (length + 1))


def cyclic_table(length):
    steps = np.arange(length)[:, None]
    column = np.arange(length)[None, :]
    freqs = (column + 1) // 2
    angles = 2.0 * np.pi * freqs * steps / length
    use_sine = (column % 2 == 0) & (column > 0)
    edges = (column == 0) | (column == length - 1)
    scales = np.where(edges, np.sqrt(1.0 / length), np.sqrt(2.0 / length))
    table = scales * np.where(use_sine, np.sin(angles), np.cos(angles))
    return table, 2.0 - 2.0 * np.cos(2.0 * np.pi * freqs[0] / length)


def pooling(fine, rows=None, columns=None):
    table = np.zeros((rows or fine, columns or fine // 2))
    table[np.arange(fine), np.arange(fine) // 2] = 1.0
    return table


def tables(doms, grps, extent):
    cx, ny, cz = extent
    x2, y2, z2 = doms * cx // 4, ny // 4, grps * cz // 4
    table_x, values_x = sine_table(x2 // 2)
    table_y, values_y = cyclic_table(y2 // 2)
    table_z, values_z = sine_table(z2 // 2)
    plane = np.kron(table_x, table_y)
    pool_xy = np.kron(pooling(x2), pooling(y2))
    pool_z = pooling(z2)
    values = values_x[:, None, None] + values_y[None, :, None] + values_z[None, None, :]
    cells = cz // 4
    spread = np.zeros((z2, cz))
    spread[np.arange(cz // 2) // 2, np.arange(cz // 2)] = 1.0
    spread[cells, cz // 2 : cz // 2 + 2] = 1.0
    spread[z2 - 1, cz - 2 :] = 1.0
    found = (
        pooling(cz, cz, cz) / 8.0,
        pooling(ny).T,
        pooling(cz // 2, cz, cz) / 8.0,
        pooling(ny // 2).T,
        (pool_xy @ plane).T / 4.0,
        pool_z @ table_z / 2.0,
        64.0 / values.reshape(-1, z2 // 2),
        pool_xy @ plane,
        (pool_z @ table_z).T,
        spread,
        pooling(ny // 2),
        pooling(cz, cz, cz).T,
        pooling(ny),
    )
    return [jnp.asarray(table, jnp.float32) for table in found]


def matmul(a, b):
    return jnp.dot(a, b, precision=HIGHEST, preferred_element_type=jnp.float32)


CORNERS = ((0, 1), (0, -1), (1, 1), (1, -1), (-1, 1), (-1, -1))


def grid_kernel(
    doms, grps,
    deposit_ref, valence_ref, start_ref,
    rz1, ry1, rz2, ry2, into_xy, into_z, inverse, from_xy, from_z, pz2, py2, pz1, py1,
    potential_ref, totals_ref,
    ua, ub, fe, spill, second, edge, faces, sides, f1, edge1, faces1, sides1, va, vb, ge,
    whole_f, wa, wb, pieces, sums,
    spill_sem, ex_send, ex_recv, ex1_send, ex1_recv, all_send, all_recv,
):
    n = doms * grps
    dom, grp = lax.axis_index("dom"), lax.axis_index("grp")
    me = dom * grps + grp
    cx, ny, cz = valence_ref.shape
    h = HALO

    def at(dx, dz):
        return (lax.rem(dom + dx + doms, doms), lax.rem(grp + dz + grps, grps))

    def nth(k):
        t = lax.rem(me + k, n)
        return (t // grps, lax.rem(t, grps))

    barrier = pltpu.get_barrier_semaphore()

    def greet(k, carry):
        pl.semaphore_signal(barrier, inc=1, device_id=nth(k), device_id_type=pl.DeviceIdType.MESH)
        return carry

    lax.fori_loop(1, n, greet, 0)
    pl.semaphore_wait(barrier, n - 1)

    def send(src, dst, send_sem, recv_sem, target):
        return pltpu.make_async_remote_copy(
            src_ref=src, dst_ref=dst, send_sem=send_sem, recv_sem=recv_sem,
            device_id=target, device_id_type=pl.DeviceIdType.MESH,
        )

    def exchange(src, planes, packed, faces_to, sides_to, send_sem, recv_sem):
        copies = [
            send(packed, sides_to.at[k], send_sem.at[k], recv_sem.at[k], at(*CORNERS[k]))
            for k in range(6)
        ]
        for k, (first, dx) in enumerate(((planes - h, 1), (0, -1))):
            part = src.at[pl.ds(first, h)]
            copies.append(send(part, faces_to.at[k], send_sem.at[6 + k], recv_sem.at[6 + k], at(dx, 0)))
        for copy in copies:
            copy.start()
        return copies

    def all_send_to(buf, which):
        def one(k):
            return send(buf.at[me], buf.at[me], all_send.at[which, k], all_recv.at[which, k], nth(k))

        def go(k, carry):
            one(k).start()
            return carry

        def done(k, carry):
            one(k).wait()
            return carry

        lax.fori_loop(1, n, go, 0)
        lax.fori_loop(1, n, done, 0)

    lane = lax.broadcasted_iota(jnp.int32, (1, cz), 1)
    edge_lane = (lane < h) | (lane >= cz - h)
    has_up = (grp < grps - 1).astype(jnp.float32)
    has_down = (grp > 0).astype(jnp.float32)
    beside = jnp.where(lane < h, has_up, 0.0) + jnp.where(lane >= cz - h, has_down, 0.0)
    lanes0 = jnp.concatenate([jnp.ones((1, cz), jnp.float32), beside], axis=1)
    half = cz // 2
    lanes1 = (
        jnp.where(lane < half, 1.0, 0.0)
        + jnp.where((lane >= half) & (lane < half + h), has_up, 0.0)
        + jnp.where(lane >= cz - h, has_down, 0.0)
    )

    def inside(plane, count):
        x = dom * count + plane - h
        return ((x >= 0) & (x < doms * count)).astype(jnp.float32)

    def pack0(src, which):
        total = jnp.zeros((ny, cz), jnp.float32)
        for x in range(cx):
            kept = jnp.where(edge_lane, src[x], 0.0)
            total = total + (kept if x == 0 else pltpu.roll(kept, 16 * x, 1))
        edge[which] = total

    def widen0(src, which, dst):
        from_up = lane % 16 < 8
        kinds = ((3, 2, 0, cx - h, 0), (1, 0, None, 0, h), (5, 4, 1, 0, cx + h))
        for up, down, face, first, place in kinds:
            mixed = jnp.where(from_up, sides[which, up], sides[which, down])
            for i in range(cx if face is None else h):
                x = first + i
                own = src[x] if face is None else faces[which, face, i]
                far = mixed if x == 0 else pltpu.roll(mixed, cz - 16 * x, 1)
                mask = inside(place + i, cx)
                dst[place + i, :, 0:cz] = own * mask
                dst[place + i, :, cz : 2 * cz] = far * (beside * mask)

    def around(u, p, axis_y, axis_z):
        c = u[p]
        total = u[p - 1] + u[p + 1]
        total = total + pltpu.roll(c, 1, 0) + pltpu.roll(c, axis_y - 1, 0)
        return c, total + pltpu.roll(c, 1, 1) + pltpu.roll(c, axis_z - 1, 1)

    def sweep0(src, dst, first, last):
        def one(p, carry):
            c, near = around(src, p, ny, 2 * cz)
            new = c * (1.0 / 3.0) + (fe[p] + near) * (1.0 / 9.0)
            dst[p] = new * (lanes0 * inside(p, cx))
            return carry

        lax.fori_loop(first, last, one, 0)

    pack0(start_ref, 0)
    going_u = exchange(start_ref, cx, edge.at[0], faces.at[0], sides.at[0], ex_send.at[0], ex_recv.at[0])
    spilling = send(
        deposit_ref.at[pl.ds(cx, cx)], spill, spill_sem.at[0], spill_sem.at[1], at(1, 0)
    )
    spilling.start()
    spilling.wait()
    inner = (dom > 0).astype(jnp.float32)
    for x in range(cx):
        second[0, x] = valence_ref[x] + (deposit_ref[x] + spill[x] * inner)
    density = second.at[0]
    pack0(density, 1)
    going_f = exchange(density, cx, edge.at[1], faces.at[1], sides.at[1], ex_send.at[1], ex_recv.at[1])
    for copy in going_u:
        copy.wait()
    widen0(start_ref, 0, ua)
    for copy in going_f:
        copy.wait()
    widen0(density, 1, fe)

    sweep0(ua, ub, 1, cx + 2 * h - 1)
    sweep0(ub, ua, 2, cx + 2 * h - 2)
    for i in range(cx // 2):
        both = jnp.zeros((ny, cz), jnp.float32)
        for p in (h + 2 * i, h + 2 * i + 1):
            c, near = around(ua, p, ny, 2 * cz)
            both = both + (fe[p] + near - 6.0 * c)[:, 0:cz]
        f1[i] = matmul(ry1[...], matmul(both, rz1[...]))

    c1, y1 = cx // 2, ny // 2
    total = jnp.zeros((y1, cz), jnp.float32)
    edge_lane1 = (lane < h) | ((lane >= half - h) & (lane < half))
    for x in range(c1):
        kept = jnp.where(edge_lane1, f1[x], 0.0)
        total = total + (kept if x == 0 else pltpu.roll(kept, 8 * x, 1))
    edge1[...] = total
    for copy in exchange(f1, c1, edge1, faces1, sides1, ex1_send, ex1_recv):
        copy.wait()
    from_up = lane < 40
    for up, down, face, first, place in ((3, 2, 0, c1 - h, 0), (1, 0, None, 0, h), (5, 4, 1, 0, c1 + h)):
        mixed = jnp.where(from_up, sides1[up], sides1[down])
        for i in range(c1 if face is None else h):
            x = first + i
            own = f1[x] if face is None else faces1[face, i]
            far = pltpu.roll(mixed, half - 8 * x, 1)
            value = jnp.where(lane < half, own, far) * (lanes1 * inside(place + i, c1))
            ge[place + i] = value
            va[place + i] = value * (4.0 / 9.0)

    def sweep1(src, dst, first, last):
        for p in range(first, last):
            c, near = around(src, p, y1, cz)
            new = c * (1.0 / 3.0) + near * (1.0 / 9.0) + ge[p] * (4.0 / 9.0)
            dst[p] = new * (lanes1 * inside(p, c1))

    sweep1(va, vb, 1, c1 + 2 * h - 1)
    packed = jnp.zeros((8, cz), jnp.float32)
    for i in range(c1 // 2):
        both = jnp.zeros((y1, cz), jnp.float32)
        for p in (h + 2 * i, h + 2 * i + 1):
            c, near = around(vb, p, y1, cz)
            both = both + (ge[p] + (near - 6.0 * c) * 0.25)
        f2 = matmul(ry2[...], matmul(both, rz2[...]))
        for k in range(2):
            j = 2 * i + k
            rows = f2[8 * k : 8 * k + 8]
            packed = packed + (rows if j == 0 else pltpu.roll(rows, 32 * j, 1))
    pieces[me] = packed
    all_send_to(pieces, 0)

    planes, y2 = 2 * doms, ny // 4
    z2 = grps * 32
    for j in range(4):
        for t in range(grps // 4):
            def unpack(d, carry):
                line = jnp.zeros((8, cz), jnp.float32)
                for g in range(4):
                    shift = 32 * ((g - j) % 4)
                    piece = pieces[d * grps + 4 * t + g]
                    piece = piece if shift == 0 else pltpu.roll(piece, shift, 1)
                    line = line + jnp.where(lane // 32 == g, piece, 0.0)
                whole_f[2 * d + j // 2, 8 * (j % 2) : 8 * (j % 2) + 8, cz * t : cz * t + cz] = line
                return carry

            lax.fori_loop(0, doms, unpack, 0)
    lane2 = lax.broadcasted_iota(jnp.int32, (1, 1, z2), 2)
    zero_plane = jnp.zeros((y2, z2), jnp.float32)
    for w in (wa, wb):
        w[0] = zero_plane
        w[planes + 1] = zero_plane

    def around2(w):
        c = w[1 : planes + 1]
        near = w[0:planes] + w[2 : planes + 2]
        near = near + pltpu.roll(c, 1, 1) + pltpu.roll(c, y2 - 1, 1)
        near = near + jnp.where(lane2 == 0, 0.0, pltpu.roll(c, 1, 2))
        return c, near + jnp.where(lane2 == z2 - 1, 0.0, pltpu.roll(c, z2 - 1, 2))

    def sweep2(src, dst):
        c, near = around2(src)
        dst[1 : planes + 1] = c * (1.0 / 3.0) + near * (1.0 / 9.0) + whole_f[...] * (16.0 / 9.0)

    wa[1 : planes + 1] = whole_f[...] * (16.0 / 9.0)
    sweep2(wa, wb)
    c, near = around2(wb)
    residue = whole_f[...] + (near - 6.0 * c) * (1.0 / 16.0)
    modes = matmul(matmul(into_xy[...], residue.reshape(planes * y2, z2)), into_z[...])
    back = matmul(matmul(from_xy[...], modes * inverse[...]), from_z[...])
    wb[1 : planes + 1] = c + back.reshape(planes, y2, z2)
    sweep2(wb, wa)
    sweep2(wa, wb)

    for i in range(c1 // 2 + 2):
        plane = wb[2 * dom + i]
        plane = pltpu.roll(plane, lax.rem(z2 - 32 * grp, z2), 1)
        fine = matmul(py2[...], matmul(plane, pz2[...]))
        for p in (2 * i + 1, 2 * i + 2):
            va[p] = (vb[p] + fine) * (lanes1 * inside(p, c1))
    sweep1(va, vb, 2, c1 + 2 * h - 2)
    sweep1(vb, va, 3, c1 + 2 * h - 3)

    for i in range(c1):
        fine = matmul(py1[...], matmul(va[h + i], pz1[...]))
        for x in (2 * i, 2 * i + 1):
            second[1, x] = ua[h + x, :, 0:cz] + fine
    update = second.at[1]
    pack0(update, 2)
    for copy in exchange(update, cx, edge.at[2], faces.at[2], sides.at[2], ex_send.at[2], ex_recv.at[2]):
        copy.wait()
    widen0(update, 2, ua)
    sweep0(ua, ub, 1, cx + 2 * h - 1)
    sweep0(ub, ua, 2, cx + 2 * h - 2)

    def grads(x, carry):
        p = x + h
        c = ua[p]
        own = c[:, 0:cz]
        potential_ref[x] = own
        grad_x = 0.5 * (ua[p + 1, :, 0:cz] - ua[p - 1, :, 0:cz])
        grad_y = 0.5 * (pltpu.roll(own, ny - 1, 0) - pltpu.roll(own, 1, 0))
        grad_z = 0.5 * (pltpu.roll(c, 2 * cz - 1, 1) - pltpu.roll(c, 1, 1))[:, 0:cz]
        pairs = (
            (grad_x, grad_x), (grad_y, grad_y), (grad_z, grad_z), (grad_y, grad_z),
            (grad_x, grad_z), (grad_x, grad_y), (own, density[x]),
        )
        return tuple(
            old + jnp.sum((a * b).reshape(ny // 8, 8, cz), axis=0)
            for old, (a, b) in zip(carry, pairs)
        )

    start = tuple(jnp.zeros((8, cz), jnp.float32) for _ in range(7))
    found = lax.fori_loop(0, cx, grads, start)
    sums[me] = jnp.concatenate(
        [jnp.sum(value, axis=0, keepdims=True) for value in found]
        + [jnp.zeros((1, cz), jnp.float32)], axis=0
    )
    all_send_to(sums, 1)
    totals_ref[...] = jnp.sum(sums[...], axis=0)


def solve_grid(deposit_grid, valence, start_potential):
    doms, grps = lax.axis_size("dom"), lax.axis_size("grp")
    n = doms * grps
    cx, ny, cz = valence.shape
    h = HALO
    c1, y1, y2, z2 = cx // 2, ny // 2, ny // 4, grps * cz // 4
    vmem = pl.BlockSpec(memory_space=pltpu.VMEM)
    constants = tables(doms, grps, valence.shape)

    def buf(*shape):
        return pltpu.VMEM(shape, jnp.float32)

    wide = buf(cx + 2 * h, ny, 2 * cz)
    wide1 = buf(c1 + 2 * h, y1, cz)
    whole = buf(2 * doms + 2, y2, z2)
    dma = pltpu.SemaphoreType.DMA
    return pl.pallas_call(
        functools.partial(grid_kernel, doms, grps),
        out_shape=(
            jax.ShapeDtypeStruct(valence.shape, jnp.float32),
            jax.ShapeDtypeStruct((8, cz), jnp.float32),
        ),
        in_specs=[vmem] * (3 + len(constants)),
        out_specs=(vmem, vmem),
        scratch_shapes=[
            wide, wide, wide, buf(cx, ny, cz), buf(2, cx, ny, cz),
            buf(3, ny, cz), buf(3, 2, h, ny, cz), buf(3, 6, ny, cz),
            buf(c1, y1, cz), buf(y1, cz), buf(2, h, y1, cz), buf(6, y1, cz),
            wide1, wide1, wide1,
            buf(2 * doms, y2, z2), whole, whole, buf(n, 8, cz), buf(n, 8, cz),
            dma((2,)), dma((3, 8)), dma((3, 8)), dma((8,)), dma((8,)), dma((2, n)), dma((2, n)),
        ],
        compiler_params=pltpu.CompilerParams(
            collective_id=0, has_side_effects=True, vmem_limit_bytes=48 * 1024 * 1024
        ),
        name="grid",
    )(deposit_grid, valence, start_potential, *constants)


def shards(
    valence,
    start_potential,
    atom_tiles,
    atom_home,
    atom_offset_x,
    atom_offset_y,
    atom_offset_z,
    atom_size,
):
    domain_count = lax.axis_size("dom")
    group_count = lax.axis_size("grp")
    device_count = domain_count * group_count
    atoms_here = atom_tiles.shape[0]
    tile_cells = atom_tiles.shape[1]
    capacity = 2 * atoms_here // device_count
    tile_index = jnp.arange(TE, dtype=jnp.int32)
    inside = tile_index[None, :] < atom_size
    inside_cube = inside[:, :, None, None] & inside[:, None, :, None] & inside[:, None, None, :]
    masked = atom_tiles * inside_cube.reshape(atom_tiles.shape).astype(jnp.float32)
    targets = jnp.arange(device_count, dtype=jnp.int32)
    matches = (atom_home == targets[None, :]).astype(jnp.int32)
    before = jnp.cumsum(matches, axis=0) - matches
    slot_rank = jnp.sum(before * matches, axis=1)
    slot_index = atom_home[:, 0] * capacity + slot_rank
    offsets = jnp.concatenate([atom_offset_x, atom_offset_y, atom_offset_z], axis=1)
    slots = device_count * capacity
    send_tiles = jnp.zeros((slots, tile_cells), jnp.float32).at[slot_index].set(masked)
    send_offsets = jnp.zeros((slots, 3), jnp.float32).at[slot_index].set(offsets.astype(jnp.float32))
    send_offsets = send_offsets.reshape(device_count, capacity, 3).transpose(0, 2, 1)
    send_offsets = jnp.pad(send_offsets, ((0, 0), (0, OFFSET_ROWS - 3), (0, 128 - capacity)))
    tile_rows = capacity * tile_cells // 128
    send = jnp.concatenate([send_tiles.reshape(device_count, tile_rows, 128), send_offsets], axis=1)
    got = lax.all_to_all(send, ("dom", "grp"), split_axis=0, concat_axis=0, tiled=True)
    got_offsets = got[:, tile_rows : tile_rows + 3, :capacity].transpose(1, 0, 2)
    got_offsets = got_offsets.reshape(-1).astype(jnp.int32)
    width_x, width_y, width_z = valence.shape
    deposit_grid = deposit(got, got_offsets, capacity, valence.shape)
    potential, partial = solve_grid(deposit_grid, valence, start_potential)
    totals = jnp.sum(partial[:7], axis=1)
    cell_count = width_x * width_y * width_z * device_count
    products = totals[:6] / cell_count
    energy = 0.5 * totals[6] / cell_count
    diagonal_mask = jnp.array([1.0, 1.0, 1.0, 0.0, 0.0, 0.0], jnp.float32)
    stress = products - energy * diagonal_mask
    return (potential, stress)


def solution(mesh):
    in_specs = (
        P("dom", None, "grp"),
        P("dom", None, "grp"),
        P(("dom", "grp"), None),
        P(("dom", "grp"), None),
        P(("dom", "grp"), None),
        P(("dom", "grp"), None),
        P(("dom", "grp"), None),
        P(("dom", "grp"), None),
    )
    out_specs = (P("dom", None, "grp"), P())
    return jax.shard_map(shards, mesh=mesh, in_specs=in_specs, out_specs=out_specs, check_vma=False)
```

```python
import jax
import jax.numpy as jnp
from jax import lax
from jax.experimental import pallas as pl
from jax.experimental.pallas import tpu as pltpu
from jax.sharding import PartitionSpec as P
import functools
import numpy as np

TE = 8
HALO = 3
HIGHEST = lax.Precision.HIGHEST


ACCS = 8
OFFSET_ROWS = 8


def parts_of(value):
    high = value.astype(jnp.bfloat16)
    rest = value - high.astype(jnp.float32)
    middle = rest.astype(jnp.bfloat16)
    low = (rest - middle.astype(jnp.float32)).astype(jnp.bfloat16)
    return high, middle, low


def times_right(rows, table):
    count = rows.shape[0]
    stacked = jnp.concatenate(parts_of(rows), axis=0)
    out = jnp.dot(stacked, table.astype(jnp.bfloat16), preferred_element_type=jnp.float32)
    return out[0:count] + (out[count : 2 * count] + out[2 * count : 3 * count])


def times_left(table, columns):
    count = columns.shape[1]
    stacked = jnp.concatenate(parts_of(columns), axis=1)
    out = jnp.dot(table.astype(jnp.bfloat16), stacked, preferred_element_type=jnp.float32)
    return out[:, 0:count] + (out[:, count : 2 * count] + out[:, 2 * count : 3 * count])


def resample(left, planes, right):
    rows = planes[0].shape[0]
    count, width = len(planes), right.shape[1]
    along = times_right(jnp.concatenate(planes, axis=0), right)
    beside = [along[rows * i : rows * i + rows] for i in range(count)]
    out = times_left(left, jnp.concatenate(beside, axis=1))
    return [out[:, width * i : width * i + width] for i in range(count)]


def swap_kernel(doms, grps, send_ref, got_ref, send_sem, recv_sem):
    n = doms * grps
    me = lax.axis_index("dom") * grps + lax.axis_index("grp")

    def copy_to(k):
        t = lax.rem(me + k, n)
        return pltpu.make_async_remote_copy(
            src_ref=send_ref.at[t], dst_ref=got_ref.at[me],
            send_sem=send_sem.at[k], recv_sem=recv_sem.at[k],
            device_id=(t // grps, lax.rem(t, grps)), device_id_type=pl.DeviceIdType.MESH,
        )

    barrier = pltpu.get_barrier_semaphore()

    def greet(k, carry):
        t = lax.rem(me + k, n)
        pl.semaphore_signal(
            barrier, inc=1, device_id=(t // grps, lax.rem(t, grps)),
            device_id_type=pl.DeviceIdType.MESH,
        )
        return carry

    def go(k, carry):
        copy_to(k).start()
        return carry

    def done(k, carry):
        copy_to(k).wait()
        return carry

    lax.fori_loop(1, n, greet, 0)
    pl.semaphore_wait(barrier, n - 1)
    lax.fori_loop(1, n, go, 0)
    got_ref[me] = send_ref[me]
    lax.fori_loop(1, n, done, 0)


def swap(send):
    doms, grps = lax.axis_size("dom"), lax.axis_size("grp")
    vmem = pl.BlockSpec(memory_space=pltpu.VMEM)
    dma = pltpu.SemaphoreType.DMA
    return pl.pallas_call(
        functools.partial(swap_kernel, doms, grps),
        out_shape=jax.ShapeDtypeStruct(send.shape, jnp.float32),
        in_specs=[vmem],
        out_specs=vmem,
        scratch_shapes=[dma((doms * grps,)), dma((doms * grps,))],
        compiler_params=pltpu.CompilerParams(
            collective_id=1, has_side_effects=True, vmem_limit_bytes=32 * 1024 * 1024
        ),
        name="swap",
    )(send)


def deposit_kernel(capacity, offsets_ref, tiles_ref, out_ref, *grids):
    slots = offsets_ref.shape[0] // 3
    width_y = out_ref.shape[1]
    lane = lax.broadcasted_iota(jnp.int32, (TE, 128), 1)
    low, high = (lane // TE == TE - 1, lane // TE == 2 * TE - 1)
    for grid in grids:
        grid[...] = jnp.zeros_like(grid)

    def step(i, carry):
        for j, grid in enumerate(grids):
            slot = i * len(grids) + j
            device = slot // capacity
            first = (slot % capacity) * 4
            at_x = offsets_ref[slot]
            at_y = width_y + TE - offsets_ref[slots + slot]
            at_z = offsets_ref[2 * slots + slot]
            parts = []
            for q in range(4):
                line = tiles_ref[device, pl.ds(first + q, 1), :]
                line = jnp.broadcast_to(line, (TE, 128))
                line = pltpu.roll(line, 0, 1, stride=TE, stride_axis=0)
                for mask, shift in ((low, (at_z + 72) % 128), (high, (at_z + 8) % 128)):
                    kept = jnp.where(mask, line, 0.0)
                    parts.append(pltpu.roll(kept, shift, 1))
            for a, part in enumerate(parts):
                spot = (at_x + a, pl.ds(at_y, TE), slice(None))
                grid[spot] = grid[spot] + part
        return carry

    lax.fori_loop(0, slots // len(grids), step, 0)
    total = grids[0][...]
    for grid in grids[1:]:
        total = total + grid[...]
    rows = grids[0].shape[1]
    held = lax.broadcasted_iota(jnp.int32, (width_y, rows), 1)
    wanted = lax.broadcasted_iota(jnp.int32, (width_y, rows), 0)
    fold = ((rows - 1 - held) % width_y == wanted).astype(jnp.float32)
    for first in range(0, out_ref.shape[0], 4):
        planes = jnp.concatenate([total[first + i] for i in range(4)], axis=1)
        folded = times_left(fold, planes)
        for i in range(4):
            out_ref[first + i] = folded[:, 128 * i : 128 * i + 128]


def deposit(tiles, offsets, capacity, extent):
    width_x, width_y, width_z = extent
    vmem = pl.BlockSpec(memory_space=pltpu.VMEM)
    return pl.pallas_call(
        functools.partial(deposit_kernel, capacity),
        out_shape=jax.ShapeDtypeStruct((width_x + TE, width_y, width_z), jnp.float32),
        in_specs=[pl.BlockSpec(memory_space=pltpu.SMEM), vmem],
        out_specs=vmem,
        scratch_shapes=[pltpu.VMEM((width_x + TE, width_y + 2 * TE, width_z), jnp.float32)] * ACCS,
        compiler_params=pltpu.CompilerParams(vmem_limit_bytes=32 * 1024 * 1024),
        name="deposit",
    )(offsets, tiles)


def sine_table(length):
    steps = np.arange(length) + 1.0
    table = np.sqrt(2.0 / (length + 1)) * np.sin(np.pi * np.outer(steps, steps) / (length + 1))
    return table, 2.0 - 2.0 * np.cos(np.pi * steps / (length + 1))


def cyclic_table(length):
    steps = np.arange(length)[:, None]
    column = np.arange(length)[None, :]
    freqs = (column + 1) // 2
    angles = 2.0 * np.pi * freqs * steps / length
    use_sine = (column % 2 == 0) & (column > 0)
    edges = (column == 0) | (column == length - 1)
    scales = np.where(edges, np.sqrt(1.0 / length), np.sqrt(2.0 / length))
    table = scales * np.where(use_sine, np.sin(angles), np.cos(angles))
    return table, 2.0 - 2.0 * np.cos(2.0 * np.pi * freqs[0] / length)


def pooling(fine, rows=None, columns=None):
    table = np.zeros((rows or fine, columns or fine // 2))
    table[np.arange(fine), np.arange(fine) // 2] = 1.0
    return table


def tables(doms, grps, extent):
    cx, ny, cz = extent
    x2, y2, z2 = doms * cx // 4, ny // 4, grps * cz // 4
    table_x, values_x = sine_table(x2 // 2)
    table_y, values_y = cyclic_table(y2 // 2)
    table_z, values_z = sine_table(z2 // 2)
    plane = np.kron(table_x, table_y)
    pool_xy = np.kron(pooling(x2), pooling(y2))
    pool_z = pooling(z2)
    values = values_x[:, None, None] + values_y[None, :, None] + values_z[None, None, :]
    cells = cz // 4
    spread = np.zeros((z2, cz))
    spread[np.arange(cz // 2) // 2, np.arange(cz // 2)] = 1.0
    spread[cells, cz // 2 : cz // 2 + 2] = 1.0
    spread[z2 - 1, cz - 2 :] = 1.0
    found = (
        pooling(cz, cz, cz) / 8.0,
        pooling(ny).T,
        pooling(cz // 2, cz, cz) / 8.0,
        pooling(ny // 2).T,
        (pool_xy @ plane).T / 4.0,
        pool_z @ table_z / 2.0,
        64.0 / values.reshape(-1, z2 // 2),
        pool_xy @ plane,
        (pool_z @ table_z).T,
        spread,
        pooling(ny // 2),
        pooling(cz, cz, cz).T,
        pooling(ny),
    )
    return [jnp.asarray(table, jnp.float32) for table in found]


def matmul(a, b):
    return jnp.dot(a, b, precision=HIGHEST, preferred_element_type=jnp.float32)


CORNERS = ((0, 1), (0, -1), (1, 1), (1, -1), (-1, 1), (-1, -1))


def grid_kernel(
    doms, grps,
    deposit_ref, valence_ref, start_ref,
    rz1, ry1, rz2, ry2, into_xy, into_z, inverse, from_xy, from_z, pz2, py2, pz1, py1,
    potential_ref, totals_ref,
    ua, ub, fe, spill, second, edge, faces, sides, f1, edge1, faces1, sides1, va, vb, ge,
    whole_f, wa, wb, pieces, sums,
    spill_sem, ex_send, ex_recv, ex1_send, ex1_recv, all_send, all_recv,
):
    n = doms * grps
    dom, grp = lax.axis_index("dom"), lax.axis_index("grp")
    me = dom * grps + grp
    cx, ny, cz = valence_ref.shape
    h = HALO

    def at(dx, dz):
        return (lax.rem(dom + dx + doms, doms), lax.rem(grp + dz + grps, grps))

    def nth(k):
        t = lax.rem(me + k, n)
        return (t // grps, lax.rem(t, grps))

    barrier = pltpu.get_barrier_semaphore()

    def greet(k, carry):
        pl.semaphore_signal(barrier, inc=1, device_id=nth(k), device_id_type=pl.DeviceIdType.MESH)
        return carry

    lax.fori_loop(1, n, greet, 0)
    pl.semaphore_wait(barrier, n - 1)

    def send(src, dst, send_sem, recv_sem, target):
        return pltpu.make_async_remote_copy(
            src_ref=src, dst_ref=dst, send_sem=send_sem, recv_sem=recv_sem,
            device_id=target, device_id_type=pl.DeviceIdType.MESH,
        )

    def exchange(src, planes, packed, faces_to, sides_to, send_sem, recv_sem):
        copies = [
            send(packed, sides_to.at[k], send_sem.at[k], recv_sem.at[k], at(*CORNERS[k]))
            for k in range(6)
        ]
        for k, (first, dx) in enumerate(((planes - h, 1), (0, -1))):
            part = src.at[pl.ds(first, h)]
            copies.append(send(part, faces_to.at[k], send_sem.at[6 + k], recv_sem.at[6 + k], at(dx, 0)))
        for copy in copies:
            copy.start()
        return copies

    def all_send_to(buf, which):
        def one(k):
            return send(buf.at[me], buf.at[me], all_send.at[which, k], all_recv.at[which, k], nth(k))

        def go(k, carry):
            one(k).start()
            return carry

        def done(k, carry):
            one(k).wait()
            return carry

        lax.fori_loop(1, n, go, 0)
        lax.fori_loop(1, n, done, 0)

    lane = lax.broadcasted_iota(jnp.int32, (1, cz), 1)
    edge_lane = (lane < h) | (lane >= cz - h)
    has_up = (grp < grps - 1).astype(jnp.float32)
    has_down = (grp > 0).astype(jnp.float32)
    beside = jnp.where(lane < h, has_up, 0.0) + jnp.where(lane >= cz - h, has_down, 0.0)
    lanes0 = jnp.concatenate([jnp.ones((1, cz), jnp.float32), beside], axis=1)
    half = cz // 2
    lanes1 = (
        jnp.where(lane < half, 1.0, 0.0)
        + jnp.where((lane >= half) & (lane < half + h), has_up, 0.0)
        + jnp.where(lane >= cz - h, has_down, 0.0)
    )

    def inside(plane, count):
        x = dom * count + plane - h
        return ((x >= 0) & (x < doms * count)).astype(jnp.float32)

    def pack0(src, which):
        total = jnp.zeros((ny, cz), jnp.float32)
        for x in range(cx):
            kept = jnp.where(edge_lane, src[x], 0.0)
            total = total + (kept if x == 0 else pltpu.roll(kept, 16 * x, 1))
        edge[which] = total

    def widen0(src, which, dst):
        from_up = lane % 16 < 8
        kinds = ((3, 2, 0, cx - h, 0), (1, 0, None, 0, h), (5, 4, 1, 0, cx + h))
        for up, down, face, first, place in kinds:
            mixed = jnp.where(from_up, sides[which, up], sides[which, down])
            for i in range(cx if face is None else h):
                x = first + i
                own = src[x] if face is None else faces[which, face, i]
                far = mixed if x == 0 else pltpu.roll(mixed, cz - 16 * x, 1)
                mask = inside(place + i, cx)
                dst[place + i, :, 0:cz] = own * mask
                dst[place + i, :, cz : 2 * cz] = far * (beside * mask)

    def around(u, p, axis_y, axis_z):
        c = u[p]
        total = u[p - 1] + u[p + 1]
        total = total + pltpu.roll(c, 1, 0) + pltpu.roll(c, axis_y - 1, 0)
        return c, total + pltpu.roll(c, 1, 1) + pltpu.roll(c, axis_z - 1, 1)

    def sweep0(src, dst, first, last):
        def one(p, carry):
            c, near = around(src, p, ny, 2 * cz)
            new = c * (1.0 / 3.0) + (fe[p] + near) * (1.0 / 9.0)
            dst[p] = new * (lanes0 * inside(p, cx))
            return carry

        lax.fori_loop(first, last, one, 0)

    pack0(start_ref, 0)
    going_u = exchange(start_ref, cx, edge.at[0], faces.at[0], sides.at[0], ex_send.at[0], ex_recv.at[0])
    spilling = send(
        deposit_ref.at[pl.ds(cx, cx)], spill, spill_sem.at[0], spill_sem.at[1], at(1, 0)
    )
    spilling.start()
    spilling.wait()
    inner = (dom > 0).astype(jnp.float32)
    for x in range(cx):
        second[0, x] = valence_ref[x] + (deposit_ref[x] + spill[x] * inner)
    density = second.at[0]
    pack0(density, 1)
    going_f = exchange(density, cx, edge.at[1], faces.at[1], sides.at[1], ex_send.at[1], ex_recv.at[1])
    for copy in going_u:
        copy.wait()
    widen0(start_ref, 0, ua)
    for copy in going_f:
        copy.wait()
    widen0(density, 1, fe)

    sweep0(ua, ub, 1, cx + 2 * h - 1)
    sweep0(ub, ua, 2, cx + 2 * h - 2)
    residues = []
    for i in range(cx // 2):
        both = jnp.zeros((ny, cz), jnp.float32)
        for p in (h + 2 * i, h + 2 * i + 1):
            c, near = around(ua, p, ny, 2 * cz)
            both = both + (fe[p] + near - 6.0 * c)[:, 0:cz]
        residues.append(both)
    for i, plane in enumerate(resample(ry1[...], residues, rz1[...])):
        f1[i] = plane

    c1, y1 = cx // 2, ny // 2
    total = jnp.zeros((y1, cz), jnp.float32)
    edge_lane1 = (lane < h) | ((lane >= half - h) & (lane < half))
    for x in range(c1):
        kept = jnp.where(edge_lane1, f1[x], 0.0)
        total = total + (kept if x == 0 else pltpu.roll(kept, 8 * x, 1))
    edge1[...] = total
    for copy in exchange(f1, c1, edge1, faces1, sides1, ex1_send, ex1_recv):
        copy.wait()
    from_up = lane < 40
    for up, down, face, first, place in ((3, 2, 0, c1 - h, 0), (1, 0, None, 0, h), (5, 4, 1, 0, c1 + h)):
        mixed = jnp.where(from_up, sides1[up], sides1[down])
        for i in range(c1 if face is None else h):
            x = first + i
            own = f1[x] if face is None else faces1[face, i]
            far = pltpu.roll(mixed, half - 8 * x, 1)
            value = jnp.where(lane < half, own, far) * (lanes1 * inside(place + i, c1))
            ge[place + i] = value
            va[place + i] = value * (4.0 / 9.0)

    def sweep1(src, dst, first, last):
        for p in range(first, last):
            c, near = around(src, p, y1, cz)
            new = c * (1.0 / 3.0) + near * (1.0 / 9.0) + ge[p] * (4.0 / 9.0)
            dst[p] = new * (lanes1 * inside(p, c1))

    sweep1(va, vb, 1, c1 + 2 * h - 1)
    packed = jnp.zeros((8, cz), jnp.float32)
    residues = []
    for i in range(c1 // 2):
        both = jnp.zeros((y1, cz), jnp.float32)
        for p in (h + 2 * i, h + 2 * i + 1):
            c, near = around(vb, p, y1, cz)
            both = both + (ge[p] + (near - 6.0 * c) * 0.25)
        residues.append(both)
    for i, f2 in enumerate(resample(ry2[...], residues, rz2[...])):
        for k in range(2):
            j = 2 * i + k
            rows = f2[8 * k : 8 * k + 8]
            packed = packed + (rows if j == 0 else pltpu.roll(rows, 32 * j, 1))
    pieces[me] = packed
    all_send_to(pieces, 0)

    planes, y2 = 2 * doms, ny // 4
    z2 = grps * 32
    for j in range(4):
        for t in range(grps // 4):
            def unpack(d, carry):
                line = jnp.zeros((8, cz), jnp.float32)
                for g in range(4):
                    shift = 32 * ((g - j) % 4)
                    piece = pieces[d * grps + 4 * t + g]
                    piece = piece if shift == 0 else pltpu.roll(piece, shift, 1)
                    line = line + jnp.where(lane // 32 == g, piece, 0.0)
                whole_f[2 * d + j // 2, 8 * (j % 2) : 8 * (j % 2) + 8, cz * t : cz * t + cz] = line
                return carry

            lax.fori_loop(0, doms, unpack, 0)
    lane2 = lax.broadcasted_iota(jnp.int32, (1, 1, z2), 2)
    zero_plane = jnp.zeros((y2, z2), jnp.float32)
    for w in (wa, wb):
        w[0] = zero_plane
        w[planes + 1] = zero_plane

    def around2(w):
        c = w[1 : planes + 1]
        near = w[0:planes] + w[2 : planes + 2]
        near = near + pltpu.roll(c, 1, 1) + pltpu.roll(c, y2 - 1, 1)
        near = near + jnp.where(lane2 == 0, 0.0, pltpu.roll(c, 1, 2))
        return c, near + jnp.where(lane2 == z2 - 1, 0.0, pltpu.roll(c, z2 - 1, 2))

    def sweep2(src, dst):
        c, near = around2(src)
        dst[1 : planes + 1] = c * (1.0 / 3.0) + near * (1.0 / 9.0) + whole_f[...] * (16.0 / 9.0)

    wa[1 : planes + 1] = whole_f[...] * (16.0 / 9.0)
    sweep2(wa, wb)
    c, near = around2(wb)
    residue = whole_f[...] + (near - 6.0 * c) * (1.0 / 16.0)
    modes = matmul(matmul(into_xy[...], residue.reshape(planes * y2, z2)), into_z[...])
    back = matmul(matmul(from_xy[...], modes * inverse[...]), from_z[...])
    wb[1 : planes + 1] = c + back.reshape(planes, y2, z2)
    sweep2(wb, wa)
    sweep2(wa, wb)

    shift = lax.rem(z2 - 32 * grp, z2)
    coarse = [pltpu.roll(wb[2 * dom + i], shift, 1) for i in range(c1 // 2 + 2)]
    for i, fine in enumerate(resample(py2[...], coarse, pz2[...])):
        for p in (2 * i + 1, 2 * i + 2):
            va[p] = (vb[p] + fine) * (lanes1 * inside(p, c1))
    sweep1(va, vb, 2, c1 + 2 * h - 2)
    sweep1(vb, va, 3, c1 + 2 * h - 3)

    coarse = [va[h + i] for i in range(c1)]
    for i, fine in enumerate(resample(py1[...], coarse, pz1[...])):
        for x in (2 * i, 2 * i + 1):
            second[1, x] = ua[h + x, :, 0:cz] + fine
    update = second.at[1]
    pack0(update, 2)
    for copy in exchange(update, cx, edge.at[2], faces.at[2], sides.at[2], ex_send.at[2], ex_recv.at[2]):
        copy.wait()
    widen0(update, 2, ua)
    sweep0(ua, ub, 1, cx + 2 * h - 1)
    sweep0(ub, ua, 2, cx + 2 * h - 2)

    def grads(x, carry):
        p = x + h
        c = ua[p]
        own = c[:, 0:cz]
        potential_ref[x] = own
        grad_x = 0.5 * (ua[p + 1, :, 0:cz] - ua[p - 1, :, 0:cz])
        grad_y = 0.5 * (pltpu.roll(own, ny - 1, 0) - pltpu.roll(own, 1, 0))
        grad_z = 0.5 * (pltpu.roll(c, 2 * cz - 1, 1) - pltpu.roll(c, 1, 1))[:, 0:cz]
        pairs = (
            (grad_x, grad_x), (grad_y, grad_y), (grad_z, grad_z), (grad_y, grad_z),
            (grad_x, grad_z), (grad_x, grad_y), (own, density[x]),
        )
        return tuple(
            old + jnp.sum((a * b).reshape(ny // 8, 8, cz), axis=0)
            for old, (a, b) in zip(carry, pairs)
        )

    start = tuple(jnp.zeros((8, cz), jnp.float32) for _ in range(7))
    found = lax.fori_loop(0, cx, grads, start)
    sums[me] = jnp.concatenate(
        [jnp.sum(value, axis=0, keepdims=True) for value in found]
        + [jnp.zeros((1, cz), jnp.float32)], axis=0
    )
    all_send_to(sums, 1)
    totals_ref[...] = jnp.sum(sums[...], axis=0)


def solve_grid(deposit_grid, valence, start_potential):
    doms, grps = lax.axis_size("dom"), lax.axis_size("grp")
    n = doms * grps
    cx, ny, cz = valence.shape
    h = HALO
    c1, y1, y2, z2 = cx // 2, ny // 2, ny // 4, grps * cz // 4
    vmem = pl.BlockSpec(memory_space=pltpu.VMEM)
    constants = tables(doms, grps, valence.shape)

    def buf(*shape):
        return pltpu.VMEM(shape, jnp.float32)

    wide = buf(cx + 2 * h, ny, 2 * cz)
    wide1 = buf(c1 + 2 * h, y1, cz)
    whole = buf(2 * doms + 2, y2, z2)
    dma = pltpu.SemaphoreType.DMA
    return pl.pallas_call(
        functools.partial(grid_kernel, doms, grps),
        out_shape=(
            jax.ShapeDtypeStruct(valence.shape, jnp.float32),
            jax.ShapeDtypeStruct((8, cz), jnp.float32),
        ),
        in_specs=[vmem] * (3 + len(constants)),
        out_specs=(vmem, vmem),
        scratch_shapes=[
            wide, wide, wide, buf(cx, ny, cz), buf(2, cx, ny, cz),
            buf(3, ny, cz), buf(3, 2, h, ny, cz), buf(3, 6, ny, cz),
            buf(c1, y1, cz), buf(y1, cz), buf(2, h, y1, cz), buf(6, y1, cz),
            wide1, wide1, wide1,
            buf(2 * doms, y2, z2), whole, whole, buf(n, 8, cz), buf(n, 8, cz),
            dma((2,)), dma((3, 8)), dma((3, 8)), dma((8,)), dma((8,)), dma((2, n)), dma((2, n)),
        ],
        compiler_params=pltpu.CompilerParams(
            collective_id=0, has_side_effects=True, vmem_limit_bytes=48 * 1024 * 1024
        ),
        name="grid",
    )(deposit_grid, valence, start_potential, *constants)


def shards(
    valence,
    start_potential,
    atom_tiles,
    atom_home,
    atom_offset_x,
    atom_offset_y,
    atom_offset_z,
    atom_size,
):
    domain_count = lax.axis_size("dom")
    group_count = lax.axis_size("grp")
    device_count = domain_count * group_count
    atoms_here = atom_tiles.shape[0]
    tile_cells = atom_tiles.shape[1]
    capacity = 2 * atoms_here // device_count
    tile_index = jnp.arange(TE, dtype=jnp.int32)
    inside = tile_index[None, :] < atom_size
    inside_cube = inside[:, :, None, None] & inside[:, None, :, None] & inside[:, None, None, :]
    masked = atom_tiles * inside_cube.reshape(atom_tiles.shape).astype(jnp.float32)
    targets = jnp.arange(device_count, dtype=jnp.int32)
    matches = (atom_home == targets[None, :]).astype(jnp.int32)
    before = jnp.cumsum(matches, axis=0) - matches
    slot_rank = jnp.sum(before * matches, axis=1)
    slot_index = atom_home[:, 0] * capacity + slot_rank
    offsets = jnp.concatenate([atom_offset_x, atom_offset_y, atom_offset_z], axis=1)
    slots = device_count * capacity
    send_tiles = jnp.zeros((slots, tile_cells), jnp.float32).at[slot_index].set(masked)
    send_offsets = jnp.zeros((slots, 3), jnp.float32).at[slot_index].set(offsets.astype(jnp.float32))
    send_offsets = send_offsets.reshape(device_count, capacity, 3).transpose(0, 2, 1)
    send_offsets = jnp.pad(send_offsets, ((0, 0), (0, OFFSET_ROWS - 3), (0, 128 - capacity)))
    tile_rows = capacity * tile_cells // 128
    send = jnp.concatenate([send_tiles.reshape(device_count, tile_rows, 128), send_offsets], axis=1)
    got = swap(send)
    got_offsets = got[:, tile_rows : tile_rows + 3, :capacity].transpose(1, 0, 2)
    got_offsets = got_offsets.reshape(-1).astype(jnp.int32)
    width_x, width_y, width_z = valence.shape
    deposit_grid = deposit(got, got_offsets, capacity, valence.shape)
    potential, partial = solve_grid(deposit_grid, valence, start_potential)
    totals = jnp.sum(partial[:7], axis=1)
    cell_count = width_x * width_y * width_z * device_count
    products = totals[:6] / cell_count
    energy = 0.5 * totals[6] / cell_count
    diagonal_mask = jnp.array([1.0, 1.0, 1.0, 0.0, 0.0, 0.0], jnp.float32)
    stress = products - energy * diagonal_mask
    return (potential, stress)


def solution(mesh):
    in_specs = (
        P("dom", None, "grp"),
        P("dom", None, "grp"),
        P(("dom", "grp"), None),
        P(("dom", "grp"), None),
        P(("dom", "grp"), None),
        P(("dom", "grp"), None),
        P(("dom", "grp"), None),
        P(("dom", "grp"), None),
    )
    out_specs = (P("dom", None, "grp"), P())
    return jax.shard_map(shards, mesh=mesh, in_specs=in_specs, out_specs=out_specs, check_vma=False)
```

```python
import jax
import jax.numpy as jnp
from jax import lax
from jax.experimental import pallas as pl
from jax.experimental.pallas import tpu as pltpu
from jax.sharding import PartitionSpec as P
import functools
import numpy as np

TE = 8
HALO = 3
HIGHEST = lax.Precision.HIGHEST


ACCS = 8
OFFSET_ROWS = 8


def parts_of(value):
    high = value.astype(jnp.bfloat16)
    rest = value - high.astype(jnp.float32)
    middle = rest.astype(jnp.bfloat16)
    low = (rest - middle.astype(jnp.float32)).astype(jnp.bfloat16)
    return high, middle, low


def times_right(rows, table):
    count = rows.shape[0]
    stacked = jnp.concatenate(parts_of(rows), axis=0)
    out = jnp.dot(stacked, table.astype(jnp.bfloat16), preferred_element_type=jnp.float32)
    return out[0:count] + (out[count : 2 * count] + out[2 * count : 3 * count])


def times_left(table, columns):
    count = columns.shape[1]
    stacked = jnp.concatenate(parts_of(columns), axis=1)
    out = jnp.dot(table.astype(jnp.bfloat16), stacked, preferred_element_type=jnp.float32)
    return out[:, 0:count] + (out[:, count : 2 * count] + out[:, 2 * count : 3 * count])


def resample(left, planes, right):
    rows = planes[0].shape[0]
    count, width = len(planes), right.shape[1]
    along = times_right(jnp.concatenate(planes, axis=0), right)
    beside = [along[rows * i : rows * i + rows] for i in range(count)]
    out = times_left(left, jnp.concatenate(beside, axis=1))
    return [out[:, width * i : width * i + width] for i in range(count)]


def swap_kernel(doms, grps, send_ref, got_ref, send_sem, recv_sem):
    n = doms * grps
    me = lax.axis_index("dom") * grps + lax.axis_index("grp")

    def copy_to(k):
        t = lax.rem(me + k, n)
        return pltpu.make_async_remote_copy(
            src_ref=send_ref.at[t], dst_ref=got_ref.at[me],
            send_sem=send_sem.at[k], recv_sem=recv_sem.at[k],
            device_id=(t // grps, lax.rem(t, grps)), device_id_type=pl.DeviceIdType.MESH,
        )

    barrier = pltpu.get_barrier_semaphore()

    def greet(k, carry):
        t = lax.rem(me + k, n)
        pl.semaphore_signal(
            barrier, inc=1, device_id=(t // grps, lax.rem(t, grps)),
            device_id_type=pl.DeviceIdType.MESH,
        )
        return carry

    def go(k, carry):
        copy_to(k).start()
        return carry

    def done(k, carry):
        copy_to(k).wait()
        return carry

    lax.fori_loop(1, n, greet, 0)
    pl.semaphore_wait(barrier, n - 1)
    lax.fori_loop(1, n, go, 0)
    got_ref[me] = send_ref[me]
    lax.fori_loop(1, n, done, 0)


def swap(send):
    doms, grps = lax.axis_size("dom"), lax.axis_size("grp")
    vmem = pl.BlockSpec(memory_space=pltpu.VMEM)
    dma = pltpu.SemaphoreType.DMA
    return pl.pallas_call(
        functools.partial(swap_kernel, doms, grps),
        out_shape=jax.ShapeDtypeStruct(send.shape, jnp.float32),
        in_specs=[vmem],
        out_specs=vmem,
        scratch_shapes=[dma((doms * grps,)), dma((doms * grps,))],
        compiler_params=pltpu.CompilerParams(
            collective_id=1, has_side_effects=True, vmem_limit_bytes=32 * 1024 * 1024
        ),
        name="swap",
    )(send)


def deposit_kernel(capacity, offsets_ref, tiles_ref, out_ref, *grids):
    slots = offsets_ref.shape[0] // 3
    width_y = out_ref.shape[1]
    lane = lax.broadcasted_iota(jnp.int32, (TE, 128), 1)
    low, high = (lane // TE == TE - 1, lane // TE == 2 * TE - 1)
    for grid in grids:
        grid[...] = jnp.zeros_like(grid)

    def step(i, carry):
        for j, grid in enumerate(grids):
            slot = i * len(grids) + j
            device = slot // capacity
            first = (slot % capacity) * 4
            at_x = offsets_ref[slot]
            at_y = width_y + TE - offsets_ref[slots + slot]
            at_z = offsets_ref[2 * slots + slot]
            parts = []
            for q in range(4):
                line = tiles_ref[device, pl.ds(first + q, 1), :]
                line = jnp.broadcast_to(line, (TE, 128))
                line = pltpu.roll(line, 0, 1, stride=TE, stride_axis=0)
                for mask, shift in ((low, (at_z + 72) % 128), (high, (at_z + 8) % 128)):
                    kept = jnp.where(mask, line, 0.0)
                    parts.append(pltpu.roll(kept, shift, 1))
            for a, part in enumerate(parts):
                spot = (at_x + a, pl.ds(at_y, TE), slice(None))
                grid[spot] = grid[spot] + part
        return carry

    lax.fori_loop(0, slots // len(grids), step, 0)
    total = grids[0][...]
    for grid in grids[1:]:
        total = total + grid[...]
    rows = grids[0].shape[1]
    held = lax.broadcasted_iota(jnp.int32, (width_y, rows), 1)
    wanted = lax.broadcasted_iota(jnp.int32, (width_y, rows), 0)
    fold = ((rows - 1 - held) % width_y == wanted).astype(jnp.float32)
    for first in range(0, out_ref.shape[0], 4):
        planes = jnp.concatenate([total[first + i] for i in range(4)], axis=1)
        folded = times_left(fold, planes)
        for i in range(4):
            out_ref[first + i] = folded[:, 128 * i : 128 * i + 128]


def deposit(tiles, offsets, capacity, extent):
    width_x, width_y, width_z = extent
    vmem = pl.BlockSpec(memory_space=pltpu.VMEM)
    return pl.pallas_call(
        functools.partial(deposit_kernel, capacity),
        out_shape=jax.ShapeDtypeStruct((width_x + TE, width_y, width_z), jnp.float32),
        in_specs=[pl.BlockSpec(memory_space=pltpu.SMEM), vmem],
        out_specs=vmem,
        scratch_shapes=[pltpu.VMEM((width_x + TE, width_y + 2 * TE, width_z), jnp.float32)] * ACCS,
        compiler_params=pltpu.CompilerParams(vmem_limit_bytes=32 * 1024 * 1024),
        name="deposit",
    )(offsets, tiles)


def sine_table(length):
    steps = np.arange(length) + 1.0
    table = np.sqrt(2.0 / (length + 1)) * np.sin(np.pi * np.outer(steps, steps) / (length + 1))
    return table, 2.0 - 2.0 * np.cos(np.pi * steps / (length + 1))


def cyclic_table(length):
    steps = np.arange(length)[:, None]
    column = np.arange(length)[None, :]
    freqs = (column + 1) // 2
    angles = 2.0 * np.pi * freqs * steps / length
    use_sine = (column % 2 == 0) & (column > 0)
    edges = (column == 0) | (column == length - 1)
    scales = np.where(edges, np.sqrt(1.0 / length), np.sqrt(2.0 / length))
    table = scales * np.where(use_sine, np.sin(angles), np.cos(angles))
    return table, 2.0 - 2.0 * np.cos(2.0 * np.pi * freqs[0] / length)


def pooling(fine, rows=None, columns=None):
    table = np.zeros((rows or fine, columns or fine // 2))
    table[np.arange(fine), np.arange(fine) // 2] = 1.0
    return table


def tables(doms, grps, extent):
    cx, ny, cz = extent
    x2, y2, z2 = doms * cx // 4, ny // 4, grps * cz // 4
    table_x, values_x = sine_table(x2 // 2)
    table_y, values_y = cyclic_table(y2 // 2)
    table_z, values_z = sine_table(z2 // 2)
    plane = np.kron(table_x, table_y)
    pool_xy = np.kron(pooling(x2), pooling(y2))
    pool_z = pooling(z2)
    values = values_x[:, None, None] + values_y[None, :, None] + values_z[None, None, :]
    cells = cz // 4
    spread = np.zeros((z2, cz))
    spread[np.arange(cz // 2) // 2, np.arange(cz // 2)] = 1.0
    spread[cells, cz // 2 : cz // 2 + 2] = 1.0
    spread[z2 - 1, cz - 2 :] = 1.0
    found = (
        pooling(cz, cz, cz) / 8.0,
        pooling(ny).T,
        pooling(cz // 2, cz, cz) / 8.0,
        pooling(ny // 2).T,
        (pool_xy @ plane).T / 4.0,
        pool_z @ table_z / 2.0,
        64.0 / values.reshape(-1, z2 // 2),
        pool_xy @ plane,
        (pool_z @ table_z).T,
        spread,
        pooling(ny // 2),
        pooling(cz, cz, cz).T,
        pooling(ny),
    )
    return [jnp.asarray(table, jnp.float32) for table in found]


def matmul(a, b):
    return jnp.dot(a, b, precision=HIGHEST, preferred_element_type=jnp.float32)


CORNERS = ((0, 1), (0, -1), (1, 1), (1, -1), (-1, 1), (-1, -1))


def grid_kernel(
    doms, grps,
    deposit_ref, valence_ref, start_ref,
    rz1, ry1, rz2, ry2, into_xy, into_z, inverse, from_xy, from_z, pz2, py2, pz1, py1,
    potential_ref, totals_ref,
    ua, ub, fe, spill, second, edge, faces, sides, f1, edge1, faces1, sides1, va, vb, ge,
    whole_f, wa, wb, pieces, sums,
    spill_sem, ex_send, ex_recv, ex1_send, ex1_recv, all_send, all_recv,
):
    n = doms * grps
    dom, grp = lax.axis_index("dom"), lax.axis_index("grp")
    me = dom * grps + grp
    cx, ny, cz = valence_ref.shape
    h = HALO

    def at(dx, dz):
        return (lax.rem(dom + dx + doms, doms), lax.rem(grp + dz + grps, grps))

    def nth(k):
        t = lax.rem(me + k, n)
        return (t // grps, lax.rem(t, grps))

    barrier = pltpu.get_barrier_semaphore()

    def greet(k, carry):
        pl.semaphore_signal(barrier, inc=1, device_id=nth(k), device_id_type=pl.DeviceIdType.MESH)
        return carry

    lax.fori_loop(1, n, greet, 0)
    pl.semaphore_wait(barrier, n - 1)

    def send(src, dst, send_sem, recv_sem, target):
        return pltpu.make_async_remote_copy(
            src_ref=src, dst_ref=dst, send_sem=send_sem, recv_sem=recv_sem,
            device_id=target, device_id_type=pl.DeviceIdType.MESH,
        )

    def exchange(src, planes, packed, faces_to, sides_to, send_sem, recv_sem):
        copies = [
            (send(packed, sides_to.at[k], send_sem.at[k], recv_sem.at[k], at(*CORNERS[k])), CORNERS[k])
            for k in range(6)
        ]
        for k, (first, dx) in enumerate(((planes - h, 1), (0, -1))):
            part = src.at[pl.ds(first, h)]
            copy = send(part, faces_to.at[k], send_sem.at[6 + k], recv_sem.at[6 + k], at(dx, 0))
            copies.append((copy, (dx, 0)))
        copies = copies[6:] + copies[:6]
        begin(copies)
        return copies

    def exists(dx, dz):
        x, z = dom + dx, grp + dz
        return (x >= 0) & (x < doms) & (z >= 0) & (z < grps)

    def begin(copies):
        for copy, (dx, dz) in copies:
            pl.when(exists(dx, dz))(copy.start)

    def finish(copies):
        for copy, (dx, dz) in copies:
            pl.when(exists(-dx, -dz))(copy.wait_recv)
            pl.when(exists(dx, dz))(copy.wait_send)

    def all_send_to(buf, which):
        def one(k):
            return send(buf.at[me], buf.at[me], all_send.at[which, k], all_recv.at[which, k], nth(k))

        def go(k, carry):
            one(k).start()
            return carry

        def done(k, carry):
            one(k).wait()
            return carry

        lax.fori_loop(1, n, go, 0)
        lax.fori_loop(1, n, done, 0)

    lane = lax.broadcasted_iota(jnp.int32, (1, cz), 1)
    edge_lane = (lane < h) | (lane >= cz - h)
    has_up = (grp < grps - 1).astype(jnp.float32)
    has_down = (grp > 0).astype(jnp.float32)
    beside = jnp.where(lane < h, has_up, 0.0) + jnp.where(lane >= cz - h, has_down, 0.0)
    lanes0 = jnp.concatenate([jnp.ones((1, cz), jnp.float32), beside], axis=1)
    half = cz // 2
    lanes1 = (
        jnp.where(lane < half, 1.0, 0.0)
        + jnp.where((lane >= half) & (lane < half + h), has_up, 0.0)
        + jnp.where(lane >= cz - h, has_down, 0.0)
    )

    def inside(plane, count):
        x = dom * count + plane - h
        return ((x >= 0) & (x < doms * count)).astype(jnp.float32)

    def pack0(src, which):
        total = jnp.zeros((ny // 2, cz), jnp.float32)
        for x in range(cx):
            kept = jnp.where(edge_lane, src[x], 0.0)
            top, bottom = kept[: ny // 2], kept[ny // 2 :]
            total = total + (top if x == 0 else pltpu.roll(top, 8 * x, 1))
            total = total + pltpu.roll(bottom, (8 * x + half) % cz, 1)
        edge[which] = total

    def widen0(src, which, dst):
        from_up = lane % 8 < 4
        kinds = ((3, 2, 0, cx - h, 0), (1, 0, None, 0, h), (5, 4, 1, 0, cx + h))
        for up, down, face, first, place in kinds:
            mixed = jnp.where(from_up, sides[which, up], sides[which, down])
            for i in range(cx if face is None else h):
                x = first + i
                own = src[x] if face is None else faces[which, face, i]
                top = mixed if x == 0 else pltpu.roll(mixed, cz - 8 * x, 1)
                bottom = pltpu.roll(mixed, (cz + half - 8 * x) % cz, 1)
                far = jnp.concatenate([top, bottom], axis=0)
                mask = inside(place + i, cx)
                if face is not None:
                    own = jnp.where(mask * jnp.ones((1, cz), jnp.float32) > 0.0, own, 0.0)
                dst[place + i, :, 0:cz] = own
                dst[place + i, :, cz : 2 * cz] = jnp.where(beside * mask > 0.0, far, 0.0)

    def around(u, p, axis_y, axis_z):
        c = u[p]
        total = u[p - 1] + u[p + 1]
        total = total + pltpu.roll(c, 1, 0) + pltpu.roll(c, axis_y - 1, 0)
        return c, total + pltpu.roll(c, 1, 1) + pltpu.roll(c, axis_z - 1, 1)

    def sweep0(src, dst, first, last):
        def one(i, carry):
            found = []
            for p in (first + 2 * i, first + 2 * i + 1):
                c, near = around(src, p, ny, 2 * cz)
                new = c * (1.0 / 3.0) + (fe[p] + near) * (1.0 / 9.0)
                found.append((p, new * (lanes0 * inside(p, cx))))
            for p, new in found:
                dst[p] = new
            return carry

        lax.fori_loop(0, (last - first) // 2, one, 0)

    reach = cx - 1
    copy = send(
        deposit_ref.at[pl.ds(cx, reach)], spill, spill_sem.at[0], spill_sem.at[1], at(1, 0)
    )
    spilling = [(copy, (1, 0))]
    begin(spilling)
    pack0(start_ref, 0)
    going_u = exchange(start_ref, cx, edge.at[0], faces.at[0], sides.at[0], ex_send.at[0], ex_recv.at[0])
    finish(spilling)
    has_spill = (dom > 0).astype(jnp.float32) * jnp.ones((1, cz), jnp.float32) > 0.0
    for x in range(cx):
        charge = deposit_ref[x]
        if x < reach:
            charge = charge + jnp.where(has_spill, spill[x], 0.0)
        second[0, x] = valence_ref[x] + charge
    density = second.at[0]
    pack0(density, 1)
    going_f = exchange(density, cx, edge.at[1], faces.at[1], sides.at[1], ex_send.at[1], ex_recv.at[1])
    finish(going_u)
    widen0(start_ref, 0, ua)
    finish(going_f)
    widen0(density, 1, fe)

    sweep0(ua, ub, 1, cx + 2 * h - 1)
    sweep0(ub, ua, 2, cx + 2 * h - 2)
    residues = []
    for i in range(cx // 2):
        both = jnp.zeros((ny, cz), jnp.float32)
        for p in (h + 2 * i, h + 2 * i + 1):
            c, near = around(ua, p, ny, 2 * cz)
            both = both + (fe[p] + near - 6.0 * c)[:, 0:cz]
        residues.append(both)
    for i, plane in enumerate(resample(ry1[...], residues, rz1[...])):
        f1[i] = plane

    c1, y1 = cx // 2, ny // 2
    total = jnp.zeros((y1, cz), jnp.float32)
    edge_lane1 = (lane < h) | ((lane >= half - h) & (lane < half))
    for x in range(c1):
        kept = jnp.where(edge_lane1, f1[x], 0.0)
        total = total + (kept if x == 0 else pltpu.roll(kept, 8 * x, 1))
    edge1[...] = total
    finish(exchange(f1, c1, edge1, faces1, sides1, ex1_send, ex1_recv))
    from_up = lane < 40
    for up, down, face, first, place in ((3, 2, 0, c1 - h, 0), (1, 0, None, 0, h), (5, 4, 1, 0, c1 + h)):
        mixed = jnp.where(from_up, sides1[up], sides1[down])
        for i in range(c1 if face is None else h):
            x = first + i
            own = f1[x] if face is None else faces1[face, i]
            far = pltpu.roll(mixed, half - 8 * x, 1)
            mask = lanes1 * inside(place + i, c1)
            value = jnp.where(mask > 0.0, jnp.where(lane < half, own, far), 0.0)
            ge[place + i] = value
            va[place + i] = value * (4.0 / 9.0)

    def sweep1(src, dst, first, last):
        for p in range(first, last):
            c, near = around(src, p, y1, cz)
            new = c * (1.0 / 3.0) + near * (1.0 / 9.0) + ge[p] * (4.0 / 9.0)
            dst[p] = new * (lanes1 * inside(p, c1))

    sweep1(va, vb, 1, c1 + 2 * h - 1)
    packed = jnp.zeros((8, cz), jnp.float32)
    residues = []
    for i in range(c1 // 2):
        both = jnp.zeros((y1, cz), jnp.float32)
        for p in (h + 2 * i, h + 2 * i + 1):
            c, near = around(vb, p, y1, cz)
            both = both + (ge[p] + (near - 6.0 * c) * 0.25)
        residues.append(both)
    for i, f2 in enumerate(resample(ry2[...], residues, rz2[...])):
        for k in range(2):
            j = 2 * i + k
            rows = f2[8 * k : 8 * k + 8]
            packed = packed + (rows if j == 0 else pltpu.roll(rows, 32 * j, 1))
    pieces[me] = packed
    all_send_to(pieces, 0)

    planes, y2 = 2 * doms, ny // 4
    z2 = grps * 32
    for j in range(4):
        for t in range(grps // 4):
            def unpack(d, carry):
                line = jnp.zeros((8, cz), jnp.float32)
                for g in range(4):
                    shift = 32 * ((g - j) % 4)
                    piece = pieces[d * grps + 4 * t + g]
                    piece = piece if shift == 0 else pltpu.roll(piece, shift, 1)
                    line = line + jnp.where(lane // 32 == g, piece, 0.0)
                whole_f[2 * d + j // 2, 8 * (j % 2) : 8 * (j % 2) + 8, cz * t : cz * t + cz] = line
                return carry

            lax.fori_loop(0, doms, unpack, 0)
    lane2 = lax.broadcasted_iota(jnp.int32, (1, 1, z2), 2)
    zero_plane = jnp.zeros((y2, z2), jnp.float32)
    for w in (wa, wb):
        w[0] = zero_plane
        w[planes + 1] = zero_plane

    def around2(w):
        c = w[1 : planes + 1]
        near = w[0:planes] + w[2 : planes + 2]
        near = near + pltpu.roll(c, 1, 1) + pltpu.roll(c, y2 - 1, 1)
        near = near + jnp.where(lane2 == 0, 0.0, pltpu.roll(c, 1, 2))
        return c, near + jnp.where(lane2 == z2 - 1, 0.0, pltpu.roll(c, z2 - 1, 2))

    def sweep2(src, dst):
        c, near = around2(src)
        dst[1 : planes + 1] = c * (1.0 / 3.0) + near * (1.0 / 9.0) + whole_f[...] * (16.0 / 9.0)

    wa[1 : planes + 1] = whole_f[...] * (16.0 / 9.0)
    sweep2(wa, wb)
    c, near = around2(wb)
    residue = whole_f[...] + (near - 6.0 * c) * (1.0 / 16.0)
    modes = matmul(matmul(into_xy[...], residue.reshape(planes * y2, z2)), into_z[...])
    back = matmul(matmul(from_xy[...], modes * inverse[...]), from_z[...])
    wb[1 : planes + 1] = c + back.reshape(planes, y2, z2)
    sweep2(wb, wa)
    sweep2(wa, wb)

    shift = lax.rem(z2 - 32 * grp, z2)
    coarse = [pltpu.roll(wb[2 * dom + i], shift, 1) for i in range(c1 // 2 + 2)]
    for i, fine in enumerate(resample(py2[...], coarse, pz2[...])):
        for p in (2 * i + 1, 2 * i + 2):
            va[p] = (vb[p] + fine) * (lanes1 * inside(p, c1))
    sweep1(va, vb, 2, c1 + 2 * h - 2)
    sweep1(vb, va, 3, c1 + 2 * h - 3)

    coarse = [va[h + i] for i in range(c1)]
    for i, fine in enumerate(resample(py1[...], coarse, pz1[...])):
        for x in (2 * i, 2 * i + 1):
            second[1, x] = ua[h + x, :, 0:cz] + fine
    update = second.at[1]
    pack0(update, 2)
    finish(exchange(update, cx, edge.at[2], faces.at[2], sides.at[2], ex_send.at[2], ex_recv.at[2]))
    widen0(update, 2, ua)
    sweep0(ua, ub, 1, cx + 2 * h - 1)
    sweep0(ub, ua, 2, cx + 2 * h - 2)

    def grads(x, carry):
        p = x + h
        c = ua[p]
        own = c[:, 0:cz]
        potential_ref[x] = own
        grad_x = 0.5 * (ua[p + 1, :, 0:cz] - ua[p - 1, :, 0:cz])
        grad_y = 0.5 * (pltpu.roll(own, ny - 1, 0) - pltpu.roll(own, 1, 0))
        grad_z = 0.5 * (pltpu.roll(c, 2 * cz - 1, 1) - pltpu.roll(c, 1, 1))[:, 0:cz]
        pairs = (
            (grad_x, grad_x), (grad_y, grad_y), (grad_z, grad_z), (grad_y, grad_z),
            (grad_x, grad_z), (grad_x, grad_y), (own, density[x]),
        )
        return tuple(
            old + jnp.sum((a * b).reshape(ny // 8, 8, cz), axis=0)
            for old, (a, b) in zip(carry, pairs)
        )

    start = tuple(jnp.zeros((8, cz), jnp.float32) for _ in range(7))
    found = lax.fori_loop(0, cx, grads, start)
    sums[me] = jnp.concatenate(
        [jnp.sum(value, axis=0, keepdims=True) for value in found]
        + [jnp.zeros((1, cz), jnp.float32)], axis=0
    )
    all_send_to(sums, 1)
    totals_ref[...] = jnp.sum(sums[...], axis=0)


def solve_grid(deposit_grid, valence, start_potential):
    doms, grps = lax.axis_size("dom"), lax.axis_size("grp")
    n = doms * grps
    cx, ny, cz = valence.shape
    h = HALO
    c1, y1, y2, z2 = cx // 2, ny // 2, ny // 4, grps * cz // 4
    vmem = pl.BlockSpec(memory_space=pltpu.VMEM)
    constants = tables(doms, grps, valence.shape)

    def buf(*shape):
        return pltpu.VMEM(shape, jnp.float32)

    wide = buf(cx + 2 * h, ny, 2 * cz)
    wide1 = buf(c1 + 2 * h, y1, cz)
    whole = buf(2 * doms + 2, y2, z2)
    dma = pltpu.SemaphoreType.DMA
    return pl.pallas_call(
        functools.partial(grid_kernel, doms, grps),
        out_shape=(
            jax.ShapeDtypeStruct(valence.shape, jnp.float32),
            jax.ShapeDtypeStruct((8, cz), jnp.float32),
        ),
        in_specs=[vmem] * (3 + len(constants)),
        out_specs=(vmem, vmem),
        scratch_shapes=[
            wide, wide, wide, buf(cx - 1, ny, cz), buf(2, cx, ny, cz),
            buf(3, ny // 2, cz), buf(3, 2, h, ny, cz), buf(3, 6, ny // 2, cz),
            buf(c1, y1, cz), buf(y1, cz), buf(2, h, y1, cz), buf(6, y1, cz),
            wide1, wide1, wide1,
            buf(2 * doms, y2, z2), whole, whole, buf(n, 8, cz), buf(n, 8, cz),
            dma((2,)), dma((3, 8)), dma((3, 8)), dma((8,)), dma((8,)), dma((2, n)), dma((2, n)),
        ],
        compiler_params=pltpu.CompilerParams(
            collective_id=0, has_side_effects=True, vmem_limit_bytes=48 * 1024 * 1024
        ),
        name="grid",
    )(deposit_grid, valence, start_potential, *constants)


def shards(
    valence,
    start_potential,
    atom_tiles,
    atom_home,
    atom_offset_x,
    atom_offset_y,
    atom_offset_z,
    atom_size,
):
    domain_count = lax.axis_size("dom")
    group_count = lax.axis_size("grp")
    device_count = domain_count * group_count
    atoms_here = atom_tiles.shape[0]
    tile_cells = atom_tiles.shape[1]
    capacity = 2 * atoms_here // device_count
    tile_index = jnp.arange(TE, dtype=jnp.int32)
    inside = tile_index[None, :] < atom_size
    inside_cube = inside[:, :, None, None] & inside[:, None, :, None] & inside[:, None, None, :]
    masked = atom_tiles * inside_cube.reshape(atom_tiles.shape).astype(jnp.float32)
    targets = jnp.arange(device_count, dtype=jnp.int32)
    matches = (atom_home == targets[None, :]).astype(jnp.int32)
    before = jnp.cumsum(matches, axis=0) - matches
    slot_rank = jnp.sum(before * matches, axis=1)
    slot_index = atom_home[:, 0] * capacity + slot_rank
    offsets = jnp.concatenate([atom_offset_x, atom_offset_y, atom_offset_z], axis=1)
    slots = device_count * capacity
    send_tiles = jnp.zeros((slots, tile_cells), jnp.float32).at[slot_index].set(masked)
    send_offsets = jnp.zeros((slots, 3), jnp.float32).at[slot_index].set(offsets.astype(jnp.float32))
    send_offsets = send_offsets.reshape(device_count, capacity, 3).transpose(0, 2, 1)
    send_offsets = jnp.pad(send_offsets, ((0, 0), (0, OFFSET_ROWS - 3), (0, 128 - capacity)))
    tile_rows = capacity * tile_cells // 128
    send = jnp.concatenate([send_tiles.reshape(device_count, tile_rows, 128), send_offsets], axis=1)
    got = swap(send)
    got_offsets = got[:, tile_rows : tile_rows + 3, :capacity].transpose(1, 0, 2)
    got_offsets = got_offsets.reshape(-1).astype(jnp.int32)
    width_x, width_y, width_z = valence.shape
    deposit_grid = deposit(got, got_offsets, capacity, valence.shape)
    potential, partial = solve_grid(deposit_grid, valence, start_potential)
    totals = jnp.sum(partial[:7], axis=1)
    cell_count = width_x * width_y * width_z * device_count
    products = totals[:6] / cell_count
    energy = 0.5 * totals[6] / cell_count
    diagonal_mask = jnp.array([1.0, 1.0, 1.0, 0.0, 0.0, 0.0], jnp.float32)
    stress = products - energy * diagonal_mask
    return (potential, stress)


def solution(mesh):
    in_specs = (
        P("dom", None, "grp"),
        P("dom", None, "grp"),
        P(("dom", "grp"), None),
        P(("dom", "grp"), None),
        P(("dom", "grp"), None),
        P(("dom", "grp"), None),
        P(("dom", "grp"), None),
        P(("dom", "grp"), None),
    )
    out_specs = (P("dom", None, "grp"), P())
    return jax.shard_map(shards, mesh=mesh, in_specs=in_specs, out_specs=out_specs, check_vma=False)
```

```python
import jax
import jax.numpy as jnp
from jax import lax
from jax.experimental import pallas as pl
from jax.experimental.pallas import tpu as pltpu
from jax.sharding import PartitionSpec as P
import functools
import numpy as np

TE = 8
HALO = 3
HIGHEST = lax.Precision.HIGHEST


ACCS = 8
OFFSET_ROWS = 8


def parts_of(value):
    high = value.astype(jnp.bfloat16)
    rest = value - high.astype(jnp.float32)
    middle = rest.astype(jnp.bfloat16)
    low = (rest - middle.astype(jnp.float32)).astype(jnp.bfloat16)
    return high, middle, low


def times_right(rows, table):
    count = rows.shape[0]
    stacked = jnp.concatenate(parts_of(rows), axis=0)
    out = jnp.dot(stacked, table.astype(jnp.bfloat16), preferred_element_type=jnp.float32)
    return out[0:count] + (out[count : 2 * count] + out[2 * count : 3 * count])


def times_left(table, columns):
    count = columns.shape[1]
    stacked = jnp.concatenate(parts_of(columns), axis=1)
    out = jnp.dot(table.astype(jnp.bfloat16), stacked, preferred_element_type=jnp.float32)
    return out[:, 0:count] + (out[:, count : 2 * count] + out[:, 2 * count : 3 * count])


def resample(left, planes, right):
    rows = planes[0].shape[0]
    count, width = len(planes), right.shape[1]
    along = times_right(jnp.concatenate(planes, axis=0), right)
    beside = [along[rows * i : rows * i + rows] for i in range(count)]
    out = times_left(left, jnp.concatenate(beside, axis=1))
    return [out[:, width * i : width * i + width] for i in range(count)]


def pack_tiles(n, capacity, info_ref, tiles_ref, send_ref):
    atoms = tiles_ref.shape[0]
    slots = n * capacity
    info = info_ref[...]
    home, size = info[:, 3:4], info[:, 4:5]
    named = lax.broadcasted_iota(jnp.int32, (atoms, n), 1) == home
    named = jnp.where(named, 1.0, 0.0)
    earlier = lax.broadcasted_iota(jnp.int32, (atoms, atoms), 1)
    earlier = earlier < lax.broadcasted_iota(jnp.int32, (atoms, atoms), 0)
    earlier = jnp.where(earlier, 1.0, 0.0).astype(jnp.bfloat16)
    before = jnp.dot(earlier, named.astype(jnp.bfloat16), preferred_element_type=jnp.float32)
    rank = jnp.sum(before * named, axis=1, keepdims=True).astype(jnp.int32)
    slot = home * capacity + rank
    place = lax.broadcasted_iota(jnp.int32, (atoms, slots), 1) == slot
    place = jnp.where(place, 1.0, 0.0).astype(jnp.bfloat16)
    first_dims = (((0,), (0,)), ((), ()))
    lane = lax.broadcasted_iota(jnp.int32, (1, 128), 1)
    for q in range(4):
        largest = jnp.maximum(2 * q + lane // 64, jnp.maximum((lane // 8) % 8, lane % 8))
        kept = jnp.where(largest < size, tiles_ref[:, 128 * q : 128 * q + 128], 0.0)
        stacked = jnp.concatenate(parts_of(kept), axis=1)
        out = lax.dot_general(place, stacked, first_dims, preferred_element_type=jnp.float32)
        out = out[:, 0:128] + (out[:, 128:256] + out[:, 256:384])
        send_ref[:, capacity * q : capacity * q + capacity, :] = out.reshape(n, capacity, 128)
    numbers = info.astype(jnp.float32).astype(jnp.bfloat16)
    rows = lax.dot_general(numbers, place, first_dims, preferred_element_type=jnp.float32)
    for d in range(n):
        tile, shift = divmod(d * capacity, 128)
        part = rows[:, 128 * tile : 128 * tile + 128]
        part = part if shift == 0 else pltpu.roll(part, 128 - shift, 1)
        send_ref[d, 4 * capacity : 4 * capacity + OFFSET_ROWS, :] = part


def swap_kernel(doms, grps, capacity, info_ref, tiles_ref, got_ref, send_ref, send_sem, recv_sem):
    n = doms * grps
    me = lax.axis_index("dom") * grps + lax.axis_index("grp")

    def copy_to(k):
        t = lax.rem(me + k, n)
        return pltpu.make_async_remote_copy(
            src_ref=send_ref.at[t], dst_ref=got_ref.at[me],
            send_sem=send_sem.at[k], recv_sem=recv_sem.at[k],
            device_id=(t // grps, lax.rem(t, grps)), device_id_type=pl.DeviceIdType.MESH,
        )

    barrier = pltpu.get_barrier_semaphore()

    def greet(k, carry):
        t = lax.rem(me + k, n)
        pl.semaphore_signal(
            barrier, inc=1, device_id=(t // grps, lax.rem(t, grps)),
            device_id_type=pl.DeviceIdType.MESH,
        )
        return carry

    def go(k, carry):
        copy_to(k).start()
        return carry

    def done(k, carry):
        copy_to(k).wait()
        return carry

    lax.fori_loop(1, n, greet, 0)
    pack_tiles(n, capacity, info_ref, tiles_ref, send_ref)
    pl.semaphore_wait(barrier, n - 1)
    lax.fori_loop(1, n, go, 0)
    got_ref[me] = send_ref[me]
    lax.fori_loop(1, n, done, 0)


def swap(info, tiles, capacity):
    doms, grps = lax.axis_size("dom"), lax.axis_size("grp")
    n = doms * grps
    vmem = pl.BlockSpec(memory_space=pltpu.VMEM)
    dma = pltpu.SemaphoreType.DMA
    shape = (n, 4 * capacity + OFFSET_ROWS, 128)
    return pl.pallas_call(
        functools.partial(swap_kernel, doms, grps, capacity),
        out_shape=jax.ShapeDtypeStruct(shape, jnp.float32),
        in_specs=[vmem, vmem],
        out_specs=vmem,
        scratch_shapes=[pltpu.VMEM(shape, jnp.float32), dma((n,)), dma((n,))],
        compiler_params=pltpu.CompilerParams(
            collective_id=1, has_side_effects=True, vmem_limit_bytes=32 * 1024 * 1024
        ),
        name="swap",
    )(info, tiles)


def deposit_kernel(capacity, offsets_ref, tiles_ref, out_ref, *grids):
    slots = offsets_ref.shape[0] // 3
    width_y = out_ref.shape[1]
    lane = lax.broadcasted_iota(jnp.int32, (TE, 128), 1)
    low, high = (lane // TE == TE - 1, lane // TE == 2 * TE - 1)
    for grid in grids:
        grid[...] = jnp.zeros_like(grid)

    def step(i, carry):
        for j, grid in enumerate(grids):
            slot = i * len(grids) + j
            device = slot // capacity
            first = slot % capacity
            at_x = offsets_ref[slot]
            at_y = width_y + TE - offsets_ref[slots + slot]
            at_z = offsets_ref[2 * slots + slot]
            parts = []
            for q in range(4):
                line = tiles_ref[device, pl.ds(q * capacity + first, 1), :]
                line = jnp.broadcast_to(line, (TE, 128))
                line = pltpu.roll(line, 0, 1, stride=TE, stride_axis=0)
                for mask, shift in ((low, (at_z + 72) % 128), (high, (at_z + 8) % 128)):
                    kept = jnp.where(mask, line, 0.0)
                    parts.append(pltpu.roll(kept, shift, 1))
            for a, part in enumerate(parts):
                spot = (at_x + a, pl.ds(at_y, TE), slice(None))
                grid[spot] = grid[spot] + part
        return carry

    lax.fori_loop(0, slots // len(grids), step, 0)
    total = grids[0][...]
    for grid in grids[1:]:
        total = total + grid[...]
    rows = grids[0].shape[1]
    held = lax.broadcasted_iota(jnp.int32, (width_y, rows), 1)
    wanted = lax.broadcasted_iota(jnp.int32, (width_y, rows), 0)
    fold = ((rows - 1 - held) % width_y == wanted).astype(jnp.float32)
    for first in range(0, out_ref.shape[0], 4):
        planes = jnp.concatenate([total[first + i] for i in range(4)], axis=1)
        folded = times_left(fold, planes)
        for i in range(4):
            out_ref[first + i] = folded[:, 128 * i : 128 * i + 128]


def deposit(tiles, offsets, capacity, extent):
    width_x, width_y, width_z = extent
    vmem = pl.BlockSpec(memory_space=pltpu.VMEM)
    return pl.pallas_call(
        functools.partial(deposit_kernel, capacity),
        out_shape=jax.ShapeDtypeStruct((width_x + TE, width_y, width_z), jnp.float32),
        in_specs=[pl.BlockSpec(memory_space=pltpu.SMEM), vmem],
        out_specs=vmem,
        scratch_shapes=[pltpu.VMEM((width_x + TE, width_y + 2 * TE, width_z), jnp.float32)] * ACCS,
        compiler_params=pltpu.CompilerParams(vmem_limit_bytes=32 * 1024 * 1024),
        name="deposit",
    )(offsets, tiles)


def sine_table(length):
    steps = np.arange(length) + 1.0
    table = np.sqrt(2.0 / (length + 1)) * np.sin(np.pi * np.outer(steps, steps) / (length + 1))
    return table, 2.0 - 2.0 * np.cos(np.pi * steps / (length + 1))


def cyclic_table(length):
    steps = np.arange(length)[:, None]
    column = np.arange(length)[None, :]
    freqs = (column + 1) // 2
    angles = 2.0 * np.pi * freqs * steps / length
    use_sine = (column % 2 == 0) & (column > 0)
    edges = (column == 0) | (column == length - 1)
    scales = np.where(edges, np.sqrt(1.0 / length), np.sqrt(2.0 / length))
    table = scales * np.where(use_sine, np.sin(angles), np.cos(angles))
    return table, 2.0 - 2.0 * np.cos(2.0 * np.pi * freqs[0] / length)


def pooling(fine, rows=None, columns=None):
    table = np.zeros((rows or fine, columns or fine // 2))
    table[np.arange(fine), np.arange(fine) // 2] = 1.0
    return table


def tables(doms, grps, extent):
    cx, ny, cz = extent
    x2, y2, z2 = doms * cx // 4, ny // 4, grps * cz // 4
    table_x, values_x = sine_table(x2 // 2)
    table_y, values_y = cyclic_table(y2 // 2)
    table_z, values_z = sine_table(z2 // 2)
    plane = np.kron(table_x, table_y)
    pool_xy = np.kron(pooling(x2), pooling(y2))
    pool_z = pooling(z2)
    values = values_x[:, None, None] + values_y[None, :, None] + values_z[None, None, :]
    cells = cz // 4
    spread = np.zeros((z2, cz))
    spread[np.arange(cz // 2) // 2, np.arange(cz // 2)] = 1.0
    spread[cells, cz // 2 : cz // 2 + 2] = 1.0
    spread[z2 - 1, cz - 2 :] = 1.0
    found = (
        pooling(cz, cz, cz) / 8.0,
        pooling(ny).T,
        pooling(cz // 2, cz, cz) / 8.0,
        pooling(ny // 2).T,
        (pool_xy @ plane).T / 4.0,
        pool_z @ table_z / 2.0,
        64.0 / values.reshape(-1, z2 // 2),
        pool_xy @ plane,
        (pool_z @ table_z).T,
        spread,
        pooling(ny // 2),
        pooling(cz, cz, cz).T,
        pooling(ny),
    )
    return [jnp.asarray(table, jnp.float32) for table in found]


def matmul(a, b):
    return jnp.dot(a, b, precision=HIGHEST, preferred_element_type=jnp.float32)


CORNERS = ((0, 1), (0, -1), (1, 1), (1, -1), (-1, 1), (-1, -1))


def grid_kernel(
    doms, grps,
    deposit_ref, valence_ref, start_ref,
    rz1, ry1, rz2, ry2, into_xy, into_z, inverse, from_xy, from_z, pz2, py2, pz1, py1,
    potential_ref, totals_ref,
    ua, ub, fe, spill, second, edge, faces, sides, f1, edge1, faces1, sides1, va, vb, ge,
    whole_f, wa, wb, pieces, sums,
    spill_sem, ex_send, ex_recv, ex1_send, ex1_recv, all_send, all_recv,
):
    n = doms * grps
    dom, grp = lax.axis_index("dom"), lax.axis_index("grp")
    me = dom * grps + grp
    cx, ny, cz = valence_ref.shape
    h = HALO

    def at(dx, dz):
        return (lax.rem(dom + dx + doms, doms), lax.rem(grp + dz + grps, grps))

    def nth(k):
        t = lax.rem(me + k, n)
        return (t // grps, lax.rem(t, grps))

    barrier = pltpu.get_barrier_semaphore()

    def greet(k, carry):
        pl.semaphore_signal(barrier, inc=1, device_id=nth(k), device_id_type=pl.DeviceIdType.MESH)
        return carry

    lax.fori_loop(1, n, greet, 0)
    pl.semaphore_wait(barrier, n - 1)

    def send(src, dst, send_sem, recv_sem, target):
        return pltpu.make_async_remote_copy(
            src_ref=src, dst_ref=dst, send_sem=send_sem, recv_sem=recv_sem,
            device_id=target, device_id_type=pl.DeviceIdType.MESH,
        )

    def exchange(src, planes, packed, faces_to, sides_to, send_sem, recv_sem):
        copies = [
            (send(packed, sides_to.at[k], send_sem.at[k], recv_sem.at[k], at(*CORNERS[k])), CORNERS[k])
            for k in range(6)
        ]
        for k, (first, dx) in enumerate(((planes - h, 1), (0, -1))):
            part = src.at[pl.ds(first, h)]
            copy = send(part, faces_to.at[k], send_sem.at[6 + k], recv_sem.at[6 + k], at(dx, 0))
            copies.append((copy, (dx, 0)))
        copies = copies[6:] + copies[:6]
        begin(copies)
        return copies

    def exists(dx, dz):
        x, z = dom + dx, grp + dz
        return (x >= 0) & (x < doms) & (z >= 0) & (z < grps)

    def begin(copies):
        for copy, (dx, dz) in copies:
            pl.when(exists(dx, dz))(copy.start)

    def finish(copies):
        for copy, (dx, dz) in copies:
            pl.when(exists(-dx, -dz))(copy.wait_recv)
            pl.when(exists(dx, dz))(copy.wait_send)

    def all_send_to(buf, which):
        def one(k):
            return send(buf.at[me], buf.at[me], all_send.at[which, k], all_recv.at[which, k], nth(k))

        def go(k, carry):
            one(k).start()
            return carry

        def done(k, carry):
            one(k).wait()
            return carry

        lax.fori_loop(1, n, go, 0)
        lax.fori_loop(1, n, done, 0)

    lane = lax.broadcasted_iota(jnp.int32, (1, cz), 1)
    edge_lane = (lane < h) | (lane >= cz - h)
    has_up = (grp < grps - 1).astype(jnp.float32)
    has_down = (grp > 0).astype(jnp.float32)
    beside = jnp.where(lane < h, has_up, 0.0) + jnp.where(lane >= cz - h, has_down, 0.0)
    lanes0 = jnp.concatenate([jnp.ones((1, cz), jnp.float32), beside], axis=1)
    half = cz // 2
    lanes1 = (
        jnp.where(lane < half, 1.0, 0.0)
        + jnp.where((lane >= half) & (lane < half + h), has_up, 0.0)
        + jnp.where(lane >= cz - h, has_down, 0.0)
    )

    def inside(plane, count):
        x = dom * count + plane - h
        return ((x >= 0) & (x < doms * count)).astype(jnp.float32)

    def pack0(src, which):
        total = jnp.zeros((ny // 2, cz), jnp.float32)
        for x in range(cx):
            kept = jnp.where(edge_lane, src[x], 0.0)
            top, bottom = kept[: ny // 2], kept[ny // 2 :]
            total = total + (top if x == 0 else pltpu.roll(top, 8 * x, 1))
            total = total + pltpu.roll(bottom, (8 * x + half) % cz, 1)
        edge[which] = total

    def widen0(src, which, dst):
        from_up = lane % 8 < 4
        kinds = ((3, 2, 0, cx - h, 0), (1, 0, None, 0, h), (5, 4, 1, 0, cx + h))
        for up, down, face, first, place in kinds:
            mixed = jnp.where(from_up, sides[which, up], sides[which, down])
            for i in range(cx if face is None else h):
                x = first + i
                own = src[x] if face is None else faces[which, face, i]
                top = mixed if x == 0 else pltpu.roll(mixed, cz - 8 * x, 1)
                bottom = pltpu.roll(mixed, (cz + half - 8 * x) % cz, 1)
                far = jnp.concatenate([top, bottom], axis=0)
                mask = inside(place + i, cx)
                if face is not None:
                    own = jnp.where(mask * jnp.ones((1, cz), jnp.float32) > 0.0, own, 0.0)
                dst[place + i, :, 0:cz] = own
                dst[place + i, :, cz : 2 * cz] = jnp.where(beside * mask > 0.0, far, 0.0)

    def around(u, p, axis_y, axis_z):
        c = u[p]
        total = u[p - 1] + u[p + 1]
        total = total + pltpu.roll(c, 1, 0) + pltpu.roll(c, axis_y - 1, 0)
        return c, total + pltpu.roll(c, 1, 1) + pltpu.roll(c, axis_z - 1, 1)

    def sweep0(src, dst, first, last):
        def one(i, carry):
            found = []
            for p in (first + 2 * i, first + 2 * i + 1):
                c, near = around(src, p, ny, 2 * cz)
                new = c * (1.0 / 3.0) + (fe[p] + near) * (1.0 / 9.0)
                found.append((p, new * (lanes0 * inside(p, cx))))
            for p, new in found:
                dst[p] = new
            return carry

        lax.fori_loop(0, (last - first) // 2, one, 0)

    reach = cx - 1
    copy = send(
        deposit_ref.at[pl.ds(cx, reach)], spill, spill_sem.at[0], spill_sem.at[1], at(1, 0)
    )
    spilling = [(copy, (1, 0))]
    begin(spilling)
    pack0(start_ref, 0)
    going_u = exchange(start_ref, cx, edge.at[0], faces.at[0], sides.at[0], ex_send.at[0], ex_recv.at[0])
    finish(spilling)
    has_spill = (dom > 0).astype(jnp.float32) * jnp.ones((1, cz), jnp.float32) > 0.0
    for x in range(cx):
        charge = deposit_ref[x]
        if x < reach:
            charge = charge + jnp.where(has_spill, spill[x], 0.0)
        second[0, x] = valence_ref[x] + charge
    density = second.at[0]
    pack0(density, 1)
    going_f = exchange(density, cx, edge.at[1], faces.at[1], sides.at[1], ex_send.at[1], ex_recv.at[1])
    finish(going_u)
    widen0(start_ref, 0, ua)
    finish(going_f)
    widen0(density, 1, fe)

    sweep0(ua, ub, 1, cx + 2 * h - 1)
    sweep0(ub, ua, 2, cx + 2 * h - 2)
    residues = []
    for i in range(cx // 2):
        both = jnp.zeros((ny, cz), jnp.float32)
        for p in (h + 2 * i, h + 2 * i + 1):
            c, near = around(ua, p, ny, 2 * cz)
            both = both + (fe[p] + near - 6.0 * c)[:, 0:cz]
        residues.append(both)
    for i, plane in enumerate(resample(ry1[...], residues, rz1[...])):
        f1[i] = plane

    c1, y1 = cx // 2, ny // 2
    total = jnp.zeros((y1, cz), jnp.float32)
    edge_lane1 = (lane < h) | ((lane >= half - h) & (lane < half))
    for x in range(c1):
        kept = jnp.where(edge_lane1, f1[x], 0.0)
        total = total + (kept if x == 0 else pltpu.roll(kept, 8 * x, 1))
    edge1[...] = total
    finish(exchange(f1, c1, edge1, faces1, sides1, ex1_send, ex1_recv))
    from_up = lane < 40
    for up, down, face, first, place in ((3, 2, 0, c1 - h, 0), (1, 0, None, 0, h), (5, 4, 1, 0, c1 + h)):
        mixed = jnp.where(from_up, sides1[up], sides1[down])
        for i in range(c1 if face is None else h):
            x = first + i
            own = f1[x] if face is None else faces1[face, i]
            far = pltpu.roll(mixed, half - 8 * x, 1)
            mask = lanes1 * inside(place + i, c1)
            value = jnp.where(mask > 0.0, jnp.where(lane < half, own, far), 0.0)
            ge[place + i] = value
            va[place + i] = value * (4.0 / 9.0)

    def sweep1(src, dst, first, last):
        for p in range(first, last):
            c, near = around(src, p, y1, cz)
            new = c * (1.0 / 3.0) + near * (1.0 / 9.0) + ge[p] * (4.0 / 9.0)
            dst[p] = new * (lanes1 * inside(p, c1))

    sweep1(va, vb, 1, c1 + 2 * h - 1)
    packed = jnp.zeros((8, cz), jnp.float32)
    residues = []
    for i in range(c1 // 2):
        both = jnp.zeros((y1, cz), jnp.float32)
        for p in (h + 2 * i, h + 2 * i + 1):
            c, near = around(vb, p, y1, cz)
            both = both + (ge[p] + (near - 6.0 * c) * 0.25)
        residues.append(both)
    for i, f2 in enumerate(resample(ry2[...], residues, rz2[...])):
        for k in range(2):
            j = 2 * i + k
            rows = f2[8 * k : 8 * k + 8]
            packed = packed + (rows if j == 0 else pltpu.roll(rows, 32 * j, 1))
    pieces[me] = packed
    all_send_to(pieces, 0)

    planes, y2 = 2 * doms, ny // 4
    z2 = grps * 32
    for j in range(4):
        for t in range(grps // 4):
            def unpack(d, carry):
                line = jnp.zeros((8, cz), jnp.float32)
                for g in range(4):
                    shift = 32 * ((g - j) % 4)
                    piece = pieces[d * grps + 4 * t + g]
                    piece = piece if shift == 0 else pltpu.roll(piece, shift, 1)
                    line = line + jnp.where(lane // 32 == g, piece, 0.0)
                whole_f[2 * d + j // 2, 8 * (j % 2) : 8 * (j % 2) + 8, cz * t : cz * t + cz] = line
                return carry

            lax.fori_loop(0, doms, unpack, 0)
    lane2 = lax.broadcasted_iota(jnp.int32, (1, 1, z2), 2)
    zero_plane = jnp.zeros((y2, z2), jnp.float32)
    for w in (wa, wb):
        w[0] = zero_plane
        w[planes + 1] = zero_plane

    def around2(w):
        c = w[1 : planes + 1]
        near = w[0:planes] + w[2 : planes + 2]
        near = near + pltpu.roll(c, 1, 1) + pltpu.roll(c, y2 - 1, 1)
        near = near + jnp.where(lane2 == 0, 0.0, pltpu.roll(c, 1, 2))
        return c, near + jnp.where(lane2 == z2 - 1, 0.0, pltpu.roll(c, z2 - 1, 2))

    def sweep2(src, dst):
        c, near = around2(src)
        dst[1 : planes + 1] = c * (1.0 / 3.0) + near * (1.0 / 9.0) + whole_f[...] * (16.0 / 9.0)

    wa[1 : planes + 1] = whole_f[...] * (16.0 / 9.0)
    sweep2(wa, wb)
    c, near = around2(wb)
    residue = whole_f[...] + (near - 6.0 * c) * (1.0 / 16.0)
    modes = matmul(matmul(into_xy[...], residue.reshape(planes * y2, z2)), into_z[...])
    back = matmul(matmul(from_xy[...], modes * inverse[...]), from_z[...])
    wb[1 : planes + 1] = c + back.reshape(planes, y2, z2)
    sweep2(wb, wa)
    sweep2(wa, wb)

    shift = lax.rem(z2 - 32 * grp, z2)
    coarse = [pltpu.roll(wb[2 * dom + i], shift, 1) for i in range(c1 // 2 + 2)]
    for i, fine in enumerate(resample(py2[...], coarse, pz2[...])):
        for p in (2 * i + 1, 2 * i + 2):
            va[p] = (vb[p] + fine) * (lanes1 * inside(p, c1))
    sweep1(va, vb, 2, c1 + 2 * h - 2)
    sweep1(vb, va, 3, c1 + 2 * h - 3)

    coarse = [va[h + i] for i in range(c1)]
    for i, fine in enumerate(resample(py1[...], coarse, pz1[...])):
        for x in (2 * i, 2 * i + 1):
            second[1, x] = ua[h + x, :, 0:cz] + fine
    update = second.at[1]
    pack0(update, 2)
    finish(exchange(update, cx, edge.at[2], faces.at[2], sides.at[2], ex_send.at[2], ex_recv.at[2]))
    widen0(update, 2, ua)
    sweep0(ua, ub, 1, cx + 2 * h - 1)
    sweep0(ub, ua, 2, cx + 2 * h - 2)

    def grads(x, carry):
        p = x + h
        c = ua[p]
        own = c[:, 0:cz]
        potential_ref[x] = own
        grad_x = 0.5 * (ua[p + 1, :, 0:cz] - ua[p - 1, :, 0:cz])
        grad_y = 0.5 * (pltpu.roll(own, ny - 1, 0) - pltpu.roll(own, 1, 0))
        grad_z = 0.5 * (pltpu.roll(c, 2 * cz - 1, 1) - pltpu.roll(c, 1, 1))[:, 0:cz]
        pairs = (
            (grad_x, grad_x), (grad_y, grad_y), (grad_z, grad_z), (grad_y, grad_z),
            (grad_x, grad_z), (grad_x, grad_y), (own, density[x]),
        )
        return tuple(
            old + jnp.sum((a * b).reshape(ny // 8, 8, cz), axis=0)
            for old, (a, b) in zip(carry, pairs)
        )

    start = tuple(jnp.zeros((8, cz), jnp.float32) for _ in range(7))
    found = lax.fori_loop(0, cx, grads, start)
    sums[me] = jnp.concatenate(
        [jnp.sum(value, axis=0, keepdims=True) for value in found]
        + [jnp.zeros((1, cz), jnp.float32)], axis=0
    )
    all_send_to(sums, 1)
    totals_ref[...] = jnp.sum(sums[...], axis=0)


def solve_grid(deposit_grid, valence, start_potential):
    doms, grps = lax.axis_size("dom"), lax.axis_size("grp")
    n = doms * grps
    cx, ny, cz = valence.shape
    h = HALO
    c1, y1, y2, z2 = cx // 2, ny // 2, ny // 4, grps * cz // 4
    vmem = pl.BlockSpec(memory_space=pltpu.VMEM)
    constants = tables(doms, grps, valence.shape)

    def buf(*shape):
        return pltpu.VMEM(shape, jnp.float32)

    wide = buf(cx + 2 * h, ny, 2 * cz)
    wide1 = buf(c1 + 2 * h, y1, cz)
    whole = buf(2 * doms + 2, y2, z2)
    dma = pltpu.SemaphoreType.DMA
    return pl.pallas_call(
        functools.partial(grid_kernel, doms, grps),
        out_shape=(
            jax.ShapeDtypeStruct(valence.shape, jnp.float32),
            jax.ShapeDtypeStruct((8, cz), jnp.float32),
        ),
        in_specs=[vmem] * (3 + len(constants)),
        out_specs=(vmem, vmem),
        scratch_shapes=[
            wide, wide, wide, buf(cx - 1, ny, cz), buf(2, cx, ny, cz),
            buf(3, ny // 2, cz), buf(3, 2, h, ny, cz), buf(3, 6, ny // 2, cz),
            buf(c1, y1, cz), buf(y1, cz), buf(2, h, y1, cz), buf(6, y1, cz),
            wide1, wide1, wide1,
            buf(2 * doms, y2, z2), whole, whole, buf(n, 8, cz), buf(n, 8, cz),
            dma((2,)), dma((3, 8)), dma((3, 8)), dma((8,)), dma((8,)), dma((2, n)), dma((2, n)),
        ],
        compiler_params=pltpu.CompilerParams(
            collective_id=0, has_side_effects=True, vmem_limit_bytes=48 * 1024 * 1024
        ),
        name="grid",
    )(deposit_grid, valence, start_potential, *constants)


def shards(
    valence,
    start_potential,
    atom_tiles,
    atom_home,
    atom_offset_x,
    atom_offset_y,
    atom_offset_z,
    atom_size,
):
    domain_count = lax.axis_size("dom")
    group_count = lax.axis_size("grp")
    device_count = domain_count * group_count
    atoms_here = atom_tiles.shape[0]
    tile_cells = atom_tiles.shape[1]
    capacity = 2 * atoms_here // device_count
    info = jnp.concatenate([atom_offset_x, atom_offset_y, atom_offset_z, atom_home, atom_size], axis=1)
    info = jnp.pad(info, ((0, 0), (0, OFFSET_ROWS - info.shape[1])))
    tile_rows = capacity * tile_cells // 128
    got = swap(info, atom_tiles, capacity)
    got_offsets = got[:, tile_rows : tile_rows + 3, :capacity].transpose(1, 0, 2)
    got_offsets = got_offsets.reshape(-1).astype(jnp.int32)
    width_x, width_y, width_z = valence.shape
    deposit_grid = deposit(got, got_offsets, capacity, valence.shape)
    potential, partial = solve_grid(deposit_grid, valence, start_potential)
    totals = jnp.sum(partial[:7], axis=1)
    cell_count = width_x * width_y * width_z * device_count
    products = totals[:6] / cell_count
    energy = 0.5 * totals[6] / cell_count
    diagonal_mask = jnp.array([1.0, 1.0, 1.0, 0.0, 0.0, 0.0], jnp.float32)
    stress = products - energy * diagonal_mask
    return (potential, stress)


def solution(mesh):
    in_specs = (
        P("dom", None, "grp"),
        P("dom", None, "grp"),
        P(("dom", "grp"), None),
        P(("dom", "grp"), None),
        P(("dom", "grp"), None),
        P(("dom", "grp"), None),
        P(("dom", "grp"), None),
        P(("dom", "grp"), None),
    )
    out_specs = (P("dom", None, "grp"), P())
    return jax.shard_map(shards, mesh=mesh, in_specs=in_specs, out_specs=out_specs, check_vma=False)
```

```python
import jax
import jax.numpy as jnp
from jax import lax
from jax.experimental import pallas as pl
from jax.experimental.pallas import tpu as pltpu
from jax.sharding import PartitionSpec as P
import functools
import numpy as np

TE = 8
HALO = 3
HIGHEST = lax.Precision.HIGHEST


ACCS = 8
OFFSET_ROWS = 8


def parts_of(value):
    high = value.astype(jnp.bfloat16)
    rest = value - high.astype(jnp.float32)
    middle = rest.astype(jnp.bfloat16)
    low = (rest - middle.astype(jnp.float32)).astype(jnp.bfloat16)
    return high, middle, low


def times_right(rows, table):
    count = rows.shape[0]
    stacked = jnp.concatenate(parts_of(rows), axis=0)
    out = jnp.dot(stacked, table.astype(jnp.bfloat16), preferred_element_type=jnp.float32)
    return out[0:count] + (out[count : 2 * count] + out[2 * count : 3 * count])


def times_left(table, columns):
    count = columns.shape[1]
    stacked = jnp.concatenate(parts_of(columns), axis=1)
    out = jnp.dot(table.astype(jnp.bfloat16), stacked, preferred_element_type=jnp.float32)
    return out[:, 0:count] + (out[:, count : 2 * count] + out[:, 2 * count : 3 * count])


def resample(left, planes, right):
    rows = planes[0].shape[0]
    count, width = len(planes), right.shape[1]
    along = times_right(jnp.concatenate(planes, axis=0), right)
    beside = [along[rows * i : rows * i + rows] for i in range(count)]
    out = times_left(left, jnp.concatenate(beside, axis=1))
    return [out[:, width * i : width * i + width] for i in range(count)]


def pack_tiles(n, capacity, info_ref, tiles_ref, send_ref):
    atoms = tiles_ref.shape[0]
    slots = n * capacity
    info = info_ref[...]
    home, size = info[:, 3:4], info[:, 4:5]
    named = lax.broadcasted_iota(jnp.int32, (atoms, n), 1) == home
    named = jnp.where(named, 1.0, 0.0)
    earlier = lax.broadcasted_iota(jnp.int32, (atoms, atoms), 1)
    earlier = earlier < lax.broadcasted_iota(jnp.int32, (atoms, atoms), 0)
    earlier = jnp.where(earlier, 1.0, 0.0).astype(jnp.bfloat16)
    before = jnp.dot(earlier, named.astype(jnp.bfloat16), preferred_element_type=jnp.float32)
    rank = jnp.sum(before * named, axis=1, keepdims=True).astype(jnp.int32)
    slot = home * capacity + rank
    place = lax.broadcasted_iota(jnp.int32, (atoms, slots), 1) == slot
    place = jnp.where(place, 1.0, 0.0).astype(jnp.bfloat16)
    first_dims = (((0,), (0,)), ((), ()))
    lane = lax.broadcasted_iota(jnp.int32, (1, 128), 1)
    for q in range(4):
        largest = jnp.maximum(2 * q + lane // 64, jnp.maximum((lane // 8) % 8, lane % 8))
        kept = jnp.where(largest < size, tiles_ref[:, 128 * q : 128 * q + 128], 0.0)
        stacked = jnp.concatenate(parts_of(kept), axis=1)
        out = lax.dot_general(place, stacked, first_dims, preferred_element_type=jnp.float32)
        out = out[:, 0:128] + (out[:, 128:256] + out[:, 256:384])
        send_ref[:, capacity * q : capacity * q + capacity, :] = out.reshape(n, capacity, 128)
    numbers = info.astype(jnp.float32).astype(jnp.bfloat16)
    rows = lax.dot_general(numbers, place, first_dims, preferred_element_type=jnp.float32)
    for d in range(n):
        tile, shift = divmod(d * capacity, 128)
        part = rows[:, 128 * tile : 128 * tile + 128]
        part = part if shift == 0 else pltpu.roll(part, 128 - shift, 1)
        send_ref[d, 4 * capacity : 4 * capacity + OFFSET_ROWS, :] = part


def swap_kernel(doms, grps, capacity, info_ref, tiles_ref, got_ref, send_ref, send_sem, recv_sem):
    n = doms * grps
    me = lax.axis_index("dom") * grps + lax.axis_index("grp")

    def copy_to(k):
        t = lax.rem(me + k, n)
        return pltpu.make_async_remote_copy(
            src_ref=send_ref.at[t], dst_ref=got_ref.at[me],
            send_sem=send_sem.at[k], recv_sem=recv_sem.at[k],
            device_id=(t // grps, lax.rem(t, grps)), device_id_type=pl.DeviceIdType.MESH,
        )

    barrier = pltpu.get_barrier_semaphore()

    def greet(k, carry):
        t = lax.rem(me + k, n)
        pl.semaphore_signal(
            barrier, inc=1, device_id=(t // grps, lax.rem(t, grps)),
            device_id_type=pl.DeviceIdType.MESH,
        )
        return carry

    def go(k, carry):
        copy_to(k).start()
        return carry

    def done(k, carry):
        copy_to(k).wait()
        return carry

    lax.fori_loop(1, n, greet, 0)
    pack_tiles(n, capacity, info_ref, tiles_ref, send_ref)
    pl.semaphore_wait(barrier, n - 1)
    lax.fori_loop(1, n, go, 0)
    got_ref[me] = send_ref[me]
    lax.fori_loop(1, n, done, 0)


def swap(info, tiles, capacity):
    doms, grps = lax.axis_size("dom"), lax.axis_size("grp")
    n = doms * grps
    vmem = pl.BlockSpec(memory_space=pltpu.VMEM)
    dma = pltpu.SemaphoreType.DMA
    shape = (n, 4 * capacity + OFFSET_ROWS, 128)
    return pl.pallas_call(
        functools.partial(swap_kernel, doms, grps, capacity),
        out_shape=jax.ShapeDtypeStruct(shape, jnp.float32),
        in_specs=[vmem, vmem],
        out_specs=vmem,
        scratch_shapes=[pltpu.VMEM(shape, jnp.float32), dma((n,)), dma((n,))],
        compiler_params=pltpu.CompilerParams(
            collective_id=1, has_side_effects=True, vmem_limit_bytes=32 * 1024 * 1024
        ),
        name="swap",
    )(info, tiles)


def deposit_kernel(capacity, offsets_ref, tiles_ref, out_ref, *grids):
    slots = offsets_ref.shape[0] // 3
    width_y = out_ref.shape[1]
    lane = lax.broadcasted_iota(jnp.int32, (TE, 128), 1)
    low, high = (lane // TE == TE - 1, lane // TE == 2 * TE - 1)
    for grid in grids:
        grid[...] = jnp.zeros_like(grid)

    def step(i, carry):
        for j, grid in enumerate(grids):
            slot = i * len(grids) + j
            device = slot // capacity
            first = slot % capacity
            at_x = offsets_ref[slot]
            at_y = width_y + TE - offsets_ref[slots + slot]
            at_z = offsets_ref[2 * slots + slot]
            parts = []
            for q in range(4):
                line = tiles_ref[device, pl.ds(q * capacity + first, 1), :]
                line = jnp.broadcast_to(line, (TE, 128))
                line = pltpu.roll(line, 0, 1, stride=TE, stride_axis=0)
                for mask, shift in ((low, (at_z + 72) % 128), (high, (at_z + 8) % 128)):
                    kept = jnp.where(mask, line, 0.0)
                    parts.append(pltpu.roll(kept, shift, 1))
            for a, part in enumerate(parts):
                spot = (at_x + a, pl.ds(at_y, TE), slice(None))
                grid[spot] = grid[spot] + part
        return carry

    lax.fori_loop(0, slots // len(grids), step, 0)
    total = grids[0][...]
    for grid in grids[1:]:
        total = total + grid[...]
    rows = grids[0].shape[1]
    held = lax.broadcasted_iota(jnp.int32, (width_y, rows), 1)
    wanted = lax.broadcasted_iota(jnp.int32, (width_y, rows), 0)
    fold = ((rows - 1 - held) % width_y == wanted).astype(jnp.float32)
    for first in range(0, out_ref.shape[0], 4):
        planes = jnp.concatenate([total[first + i] for i in range(4)], axis=1)
        folded = times_left(fold, planes)
        for i in range(4):
            out_ref[first + i] = folded[:, 128 * i : 128 * i + 128]


def deposit(tiles, offsets, capacity, extent):
    width_x, width_y, width_z = extent
    vmem = pl.BlockSpec(memory_space=pltpu.VMEM)
    return pl.pallas_call(
        functools.partial(deposit_kernel, capacity),
        out_shape=jax.ShapeDtypeStruct((width_x + TE, width_y, width_z), jnp.float32),
        in_specs=[pl.BlockSpec(memory_space=pltpu.SMEM), vmem],
        out_specs=vmem,
        scratch_shapes=[pltpu.VMEM((width_x + TE, width_y + 2 * TE, width_z), jnp.float32)] * ACCS,
        compiler_params=pltpu.CompilerParams(vmem_limit_bytes=32 * 1024 * 1024),
        name="deposit",
    )(offsets, tiles)


def sine_table(length):
    steps = np.arange(length) + 1.0
    table = np.sqrt(2.0 / (length + 1)) * np.sin(np.pi * np.outer(steps, steps) / (length + 1))
    return table, 2.0 - 2.0 * np.cos(np.pi * steps / (length + 1))


def cyclic_table(length):
    steps = np.arange(length)[:, None]
    column = np.arange(length)[None, :]
    freqs = (column + 1) // 2
    angles = 2.0 * np.pi * freqs * steps / length
    use_sine = (column % 2 == 0) & (column > 0)
    edges = (column == 0) | (column == length - 1)
    scales = np.where(edges, np.sqrt(1.0 / length), np.sqrt(2.0 / length))
    table = scales * np.where(use_sine, np.sin(angles), np.cos(angles))
    return table, 2.0 - 2.0 * np.cos(2.0 * np.pi * freqs[0] / length)


def pooling(fine, rows=None, columns=None):
    table = np.zeros((rows or fine, columns or fine // 2))
    table[np.arange(fine), np.arange(fine) // 2] = 1.0
    return table


def tables(doms, grps, extent):
    cx, ny, cz = extent
    x2, y2, z2 = doms * cx // 4, ny // 4, grps * cz // 4
    table_x, values_x = sine_table(x2 // 2)
    table_y, values_y = cyclic_table(y2 // 2)
    table_z, values_z = sine_table(z2 // 2)
    plane = np.kron(table_x, table_y)
    pool_xy = np.kron(pooling(x2), pooling(y2))
    pool_z = pooling(z2)
    values = values_x[:, None, None] + values_y[None, :, None] + values_z[None, None, :]
    cells = cz // 4
    spread = np.zeros((z2, cz))
    spread[np.arange(cz // 2) // 2, np.arange(cz // 2)] = 1.0
    spread[cells, cz // 2 : cz // 2 + 2] = 1.0
    spread[z2 - 1, cz - 2 :] = 1.0
    found = (
        pooling(cz, cz, cz) / 8.0,
        pooling(ny).T,
        pooling(cz // 2, cz, cz) / 8.0,
        pooling(ny // 2).T,
        (pool_xy @ plane).T / 4.0,
        pool_z @ table_z / 2.0,
        64.0 / values.reshape(-1, z2 // 2),
        pool_xy @ plane,
        (pool_z @ table_z).T,
        spread,
        pooling(ny // 2),
        pooling(cz, cz, cz).T,
        pooling(ny),
    )
    return [jnp.asarray(table, jnp.float32) for table in found]


def matmul(a, b):
    return jnp.dot(a, b, precision=HIGHEST, preferred_element_type=jnp.float32)


CORNERS = ((0, 1), (0, -1), (1, 1), (1, -1), (-1, 1), (-1, -1))


def grid_kernel(
    doms, grps,
    deposit_ref, valence_ref, start_ref,
    rz1, ry1, rz2, ry2, into_xy, into_z, inverse, from_xy, from_z, pz2, py2, pz1, py1,
    potential_ref, totals_ref,
    ua, ub, fe, spill, second, edge, faces, sides, f1, edge1, faces1, sides1, va, vb, ge,
    whole_f, wa, wb, pieces, sums,
    spill_sem, ex_send, ex_recv, ex1_send, ex1_recv, all_send, all_recv,
):
    n = doms * grps
    dom, grp = lax.axis_index("dom"), lax.axis_index("grp")
    me = dom * grps + grp
    cx, ny, cz = valence_ref.shape
    h = HALO

    def at(dx, dz):
        return (lax.rem(dom + dx + doms, doms), lax.rem(grp + dz + grps, grps))

    def nth(k):
        t = lax.rem(me + k, n)
        return (t // grps, lax.rem(t, grps))

    barrier = pltpu.get_barrier_semaphore()

    def greet(k, carry):
        pl.semaphore_signal(barrier, inc=1, device_id=nth(k), device_id_type=pl.DeviceIdType.MESH)
        return carry

    lax.fori_loop(1, n, greet, 0)
    pl.semaphore_wait(barrier, n - 1)

    def send(src, dst, send_sem, recv_sem, target):
        return pltpu.make_async_remote_copy(
            src_ref=src, dst_ref=dst, send_sem=send_sem, recv_sem=recv_sem,
            device_id=target, device_id_type=pl.DeviceIdType.MESH,
        )

    def exchange(src, planes, packed, faces_to, sides_to, send_sem, recv_sem):
        copies = [
            (send(packed, sides_to.at[k], send_sem.at[k], recv_sem.at[k], at(*CORNERS[k])), CORNERS[k])
            for k in range(6)
        ]
        for k, (first, dx) in enumerate(((planes - h, 1), (0, -1))):
            part = src.at[pl.ds(first, h)]
            copy = send(part, faces_to.at[k], send_sem.at[6 + k], recv_sem.at[6 + k], at(dx, 0))
            copies.append((copy, (dx, 0)))
        copies = copies[6:] + copies[:6]
        begin(copies)
        return copies

    def exists(dx, dz):
        x, z = dom + dx, grp + dz
        return (x >= 0) & (x < doms) & (z >= 0) & (z < grps)

    def begin(copies):
        for copy, (dx, dz) in copies:
            pl.when(exists(dx, dz))(copy.start)

    def finish(copies):
        for copy, (dx, dz) in copies:
            pl.when(exists(-dx, -dz))(copy.wait_recv)
            pl.when(exists(dx, dz))(copy.wait_send)

    def all_send_to(buf, which):
        def one(k):
            return send(buf.at[me], buf.at[me], all_send.at[which, k], all_recv.at[which, k], nth(k))

        def go(k, carry):
            one(k).start()
            return carry

        def done(k, carry):
            one(k).wait()
            return carry

        lax.fori_loop(1, n, go, 0)
        lax.fori_loop(1, n, done, 0)

    lane = lax.broadcasted_iota(jnp.int32, (1, cz), 1)
    edge_lane = (lane < h) | (lane >= cz - h)
    has_up = (grp < grps - 1).astype(jnp.float32)
    has_down = (grp > 0).astype(jnp.float32)
    beside = jnp.where(lane < h, has_up, 0.0) + jnp.where(lane >= cz - h, has_down, 0.0)
    lanes0 = jnp.concatenate([jnp.ones((1, cz), jnp.float32), beside], axis=1)
    half = cz // 2
    lanes1 = (
        jnp.where(lane < half, 1.0, 0.0)
        + jnp.where((lane >= half) & (lane < half + h), has_up, 0.0)
        + jnp.where(lane >= cz - h, has_down, 0.0)
    )

    def inside(plane, count):
        x = dom * count + plane - h
        return ((x >= 0) & (x < doms * count)).astype(jnp.float32)

    def pack0(src, which):
        total = jnp.zeros((ny // 2, cz), jnp.float32)
        for x in range(cx):
            kept = jnp.where(edge_lane, src[x], 0.0)
            top, bottom = kept[: ny // 2], kept[ny // 2 :]
            total = total + (top if x == 0 else pltpu.roll(top, 8 * x, 1))
            total = total + pltpu.roll(bottom, (8 * x + half) % cz, 1)
        edge[which] = total

    def widen0(src, which, dst):
        from_up = lane % 8 < 4
        kinds = ((3, 2, 0, cx - h, 0), (1, 0, None, 0, h), (5, 4, 1, 0, cx + h))
        for up, down, face, first, place in kinds:
            mixed = jnp.where(from_up, sides[which, up], sides[which, down])
            for i in range(cx if face is None else h):
                x = first + i
                own = src[x] if face is None else faces[which, face, i]
                top = mixed if x == 0 else pltpu.roll(mixed, cz - 8 * x, 1)
                bottom = pltpu.roll(mixed, (cz + half - 8 * x) % cz, 1)
                far = jnp.concatenate([top, bottom], axis=0)
                mask = inside(place + i, cx)
                if face is not None:
                    own = jnp.where(mask * jnp.ones((1, cz), jnp.float32) > 0.0, own, 0.0)
                dst[place + i, :, 0:cz] = own
                dst[place + i, :, cz : 2 * cz] = jnp.where(beside * mask > 0.0, far, 0.0)

    def around(u, p, axis_y, axis_z):
        c = u[p]
        total = u[p - 1] + u[p + 1]
        total = total + pltpu.roll(c, 1, 0) + pltpu.roll(c, axis_y - 1, 0)
        return c, total + pltpu.roll(c, 1, 1) + pltpu.roll(c, axis_z - 1, 1)

    def sweep0(src, dst, first, last):
        count = (last - first) // 2

        def one(i, carry):
            for p in [first + count * i + k for k in range(count)]:
                c, near = around(src, p, ny, 2 * cz)
                new = c * (1.0 / 3.0) + (fe[p] + near) * (1.0 / 9.0)
                dst[p] = new * (lanes0 * inside(p, cx))
            return carry

        lax.fori_loop(0, 2, one, 0)

    reach = cx - 1
    copy = send(
        deposit_ref.at[pl.ds(cx, reach)], spill, spill_sem.at[0], spill_sem.at[1], at(1, 0)
    )
    spilling = [(copy, (1, 0))]
    begin(spilling)
    pack0(start_ref, 0)
    going_u = exchange(start_ref, cx, edge.at[0], faces.at[0], sides.at[0], ex_send.at[0], ex_recv.at[0])
    finish(spilling)
    has_spill = (dom > 0).astype(jnp.float32) * jnp.ones((1, cz), jnp.float32) > 0.0
    for x in range(cx):
        charge = deposit_ref[x]
        if x < reach:
            charge = charge + jnp.where(has_spill, spill[x], 0.0)
        second[0, x] = valence_ref[x] + charge
    density = second.at[0]
    pack0(density, 1)
    going_f = exchange(density, cx, edge.at[1], faces.at[1], sides.at[1], ex_send.at[1], ex_recv.at[1])
    finish(going_u)
    widen0(start_ref, 0, ua)
    finish(going_f)
    widen0(density, 1, fe)

    sweep0(ua, ub, 1, cx + 2 * h - 1)
    sweep0(ub, ua, 2, cx + 2 * h - 2)
    residues = []
    for i in range(cx // 2):
        both = jnp.zeros((ny, cz), jnp.float32)
        for p in (h + 2 * i, h + 2 * i + 1):
            c, near = around(ua, p, ny, 2 * cz)
            both = both + (fe[p] + near - 6.0 * c)[:, 0:cz]
        residues.append(both)
    for i, plane in enumerate(resample(ry1[...], residues, rz1[...])):
        f1[i] = plane

    c1, y1 = cx // 2, ny // 2
    total = jnp.zeros((y1, cz), jnp.float32)
    edge_lane1 = (lane < h) | ((lane >= half - h) & (lane < half))
    for x in range(c1):
        kept = jnp.where(edge_lane1, f1[x], 0.0)
        total = total + (kept if x == 0 else pltpu.roll(kept, 8 * x, 1))
    edge1[...] = total
    finish(exchange(f1, c1, edge1, faces1, sides1, ex1_send, ex1_recv))
    from_up = lane < 40
    for up, down, face, first, place in ((3, 2, 0, c1 - h, 0), (1, 0, None, 0, h), (5, 4, 1, 0, c1 + h)):
        mixed = jnp.where(from_up, sides1[up], sides1[down])
        for i in range(c1 if face is None else h):
            x = first + i
            own = f1[x] if face is None else faces1[face, i]
            far = pltpu.roll(mixed, half - 8 * x, 1)
            mask = lanes1 * inside(place + i, c1)
            value = jnp.where(mask > 0.0, jnp.where(lane < half, own, far), 0.0)
            ge[place + i] = value
            va[place + i] = value * (4.0 / 9.0)

    def sweep1(src, dst, first, last):
        for p in range(first, last):
            c, near = around(src, p, y1, cz)
            new = c * (1.0 / 3.0) + near * (1.0 / 9.0) + ge[p] * (4.0 / 9.0)
            dst[p] = new * (lanes1 * inside(p, c1))

    sweep1(va, vb, 1, c1 + 2 * h - 1)
    packed = jnp.zeros((8, cz), jnp.float32)
    residues = []
    for i in range(c1 // 2):
        both = jnp.zeros((y1, cz), jnp.float32)
        for p in (h + 2 * i, h + 2 * i + 1):
            c, near = around(vb, p, y1, cz)
            both = both + (ge[p] + (near - 6.0 * c) * 0.25)
        residues.append(both)
    for i, f2 in enumerate(resample(ry2[...], residues, rz2[...])):
        for k in range(2):
            j = 2 * i + k
            rows = f2[8 * k : 8 * k + 8]
            packed = packed + (rows if j == 0 else pltpu.roll(rows, 32 * j, 1))
    pieces[me] = packed
    all_send_to(pieces, 0)

    planes, y2 = 2 * doms, ny // 4
    z2 = grps * 32
    for j in range(4):
        for t in range(grps // 4):
            def unpack(d, carry):
                line = jnp.zeros((8, cz), jnp.float32)
                for g in range(4):
                    shift = 32 * ((g - j) % 4)
                    piece = pieces[d * grps + 4 * t + g]
                    piece = piece if shift == 0 else pltpu.roll(piece, shift, 1)
                    line = line + jnp.where(lane // 32 == g, piece, 0.0)
                whole_f[2 * d + j // 2, 8 * (j % 2) : 8 * (j % 2) + 8, cz * t : cz * t + cz] = line
                return carry

            lax.fori_loop(0, doms, unpack, 0)
    lane2 = lax.broadcasted_iota(jnp.int32, (1, 1, z2), 2)
    zero_plane = jnp.zeros((y2, z2), jnp.float32)
    for w in (wa, wb):
        w[0] = zero_plane
        w[planes + 1] = zero_plane

    def around2(w):
        c = w[1 : planes + 1]
        near = w[0:planes] + w[2 : planes + 2]
        near = near + pltpu.roll(c, 1, 1) + pltpu.roll(c, y2 - 1, 1)
        near = near + jnp.where(lane2 == 0, 0.0, pltpu.roll(c, 1, 2))
        return c, near + jnp.where(lane2 == z2 - 1, 0.0, pltpu.roll(c, z2 - 1, 2))

    def sweep2(src, dst):
        c, near = around2(src)
        dst[1 : planes + 1] = c * (1.0 / 3.0) + near * (1.0 / 9.0) + whole_f[...] * (16.0 / 9.0)

    wa[1 : planes + 1] = whole_f[...] * (16.0 / 9.0)
    sweep2(wa, wb)
    c, near = around2(wb)
    residue = whole_f[...] + (near - 6.0 * c) * (1.0 / 16.0)
    modes = matmul(matmul(into_xy[...], residue.reshape(planes * y2, z2)), into_z[...])
    back = matmul(matmul(from_xy[...], modes * inverse[...]), from_z[...])
    wb[1 : planes + 1] = c + back.reshape(planes, y2, z2)
    sweep2(wb, wa)
    sweep2(wa, wb)

    shift = lax.rem(z2 - 32 * grp, z2)
    coarse = [pltpu.roll(wb[2 * dom + i], shift, 1) for i in range(c1 // 2 + 2)]
    for i, fine in enumerate(resample(py2[...], coarse, pz2[...])):
        for p in (2 * i + 1, 2 * i + 2):
            va[p] = (vb[p] + fine) * (lanes1 * inside(p, c1))
    sweep1(va, vb, 2, c1 + 2 * h - 2)
    sweep1(vb, va, 3, c1 + 2 * h - 3)

    coarse = [va[h + i] for i in range(c1)]
    for i, fine in enumerate(resample(py1[...], coarse, pz1[...])):
        for x in (2 * i, 2 * i + 1):
            second[1, x] = ua[h + x, :, 0:cz] + fine
    update = second.at[1]
    pack0(update, 2)
    finish(exchange(update, cx, edge.at[2], faces.at[2], sides.at[2], ex_send.at[2], ex_recv.at[2]))
    widen0(update, 2, ua)
    sweep0(ua, ub, 1, cx + 2 * h - 1)
    sweep0(ub, ua, 2, cx + 2 * h - 2)

    def grads(x, carry):
        p = x + h
        c = ua[p]
        own = c[:, 0:cz]
        potential_ref[x] = own
        grad_x = 0.5 * (ua[p + 1, :, 0:cz] - ua[p - 1, :, 0:cz])
        grad_y = 0.5 * (pltpu.roll(own, ny - 1, 0) - pltpu.roll(own, 1, 0))
        grad_z = 0.5 * (pltpu.roll(c, 2 * cz - 1, 1) - pltpu.roll(c, 1, 1))[:, 0:cz]
        pairs = (
            (grad_x, grad_x), (grad_y, grad_y), (grad_z, grad_z), (grad_y, grad_z),
            (grad_x, grad_z), (grad_x, grad_y), (own, density[x]),
        )
        return tuple(
            old + jnp.sum((a * b).reshape(ny // 8, 8, cz), axis=0)
            for old, (a, b) in zip(carry, pairs)
        )

    start = tuple(jnp.zeros((8, cz), jnp.float32) for _ in range(7))
    found = lax.fori_loop(0, cx, grads, start)
    sums[me] = jnp.concatenate(
        [jnp.sum(value, axis=0, keepdims=True) for value in found]
        + [jnp.zeros((1, cz), jnp.float32)], axis=0
    )
    all_send_to(sums, 1)
    totals_ref[...] = jnp.sum(sums[...], axis=0)


def solve_grid(deposit_grid, valence, start_potential):
    doms, grps = lax.axis_size("dom"), lax.axis_size("grp")
    n = doms * grps
    cx, ny, cz = valence.shape
    h = HALO
    c1, y1, y2, z2 = cx // 2, ny // 2, ny // 4, grps * cz // 4
    vmem = pl.BlockSpec(memory_space=pltpu.VMEM)
    constants = tables(doms, grps, valence.shape)

    def buf(*shape):
        return pltpu.VMEM(shape, jnp.float32)

    wide = buf(cx + 2 * h, ny, 2 * cz)
    wide1 = buf(c1 + 2 * h, y1, cz)
    whole = buf(2 * doms + 2, y2, z2)
    dma = pltpu.SemaphoreType.DMA
    return pl.pallas_call(
        functools.partial(grid_kernel, doms, grps),
        out_shape=(
            jax.ShapeDtypeStruct(valence.shape, jnp.float32),
            jax.ShapeDtypeStruct((8, cz), jnp.float32),
        ),
        in_specs=[vmem] * (3 + len(constants)),
        out_specs=(vmem, vmem),
        scratch_shapes=[
            wide, wide, wide, buf(cx - 1, ny, cz), buf(2, cx, ny, cz),
            buf(3, ny // 2, cz), buf(3, 2, h, ny, cz), buf(3, 6, ny // 2, cz),
            buf(c1, y1, cz), buf(y1, cz), buf(2, h, y1, cz), buf(6, y1, cz),
            wide1, wide1, wide1,
            buf(2 * doms, y2, z2), whole, whole, buf(n, 8, cz), buf(n, 8, cz),
            dma((2,)), dma((3, 8)), dma((3, 8)), dma((8,)), dma((8,)), dma((2, n)), dma((2, n)),
        ],
        compiler_params=pltpu.CompilerParams(
            collective_id=0, has_side_effects=True, vmem_limit_bytes=48 * 1024 * 1024
        ),
        name="grid",
    )(deposit_grid, valence, start_potential, *constants)


def shards(
    valence,
    start_potential,
    atom_tiles,
    atom_home,
    atom_offset_x,
    atom_offset_y,
    atom_offset_z,
    atom_size,
):
    domain_count = lax.axis_size("dom")
    group_count = lax.axis_size("grp")
    device_count = domain_count * group_count
    atoms_here = atom_tiles.shape[0]
    tile_cells = atom_tiles.shape[1]
    capacity = 2 * atoms_here // device_count
    info = jnp.concatenate([atom_offset_x, atom_offset_y, atom_offset_z, atom_home, atom_size], axis=1)
    info = jnp.pad(info, ((0, 0), (0, OFFSET_ROWS - info.shape[1])))
    tile_rows = capacity * tile_cells // 128
    got = swap(info, atom_tiles, capacity)
    got_offsets = got[:, tile_rows : tile_rows + 3, :capacity].transpose(1, 0, 2)
    got_offsets = got_offsets.reshape(-1).astype(jnp.int32)
    width_x, width_y, width_z = valence.shape
    deposit_grid = deposit(got, got_offsets, capacity, valence.shape)
    potential, partial = solve_grid(deposit_grid, valence, start_potential)
    totals = jnp.sum(partial[:7], axis=1)
    cell_count = width_x * width_y * width_z * device_count
    products = totals[:6] / cell_count
    energy = 0.5 * totals[6] / cell_count
    diagonal_mask = jnp.array([1.0, 1.0, 1.0, 0.0, 0.0, 0.0], jnp.float32)
    stress = products - energy * diagonal_mask
    return (potential, stress)


def solution(mesh):
    in_specs = (
        P("dom", None, "grp"),
        P("dom", None, "grp"),
        P(("dom", "grp"), None),
        P(("dom", "grp"), None),
        P(("dom", "grp"), None),
        P(("dom", "grp"), None),
        P(("dom", "grp"), None),
        P(("dom", "grp"), None),
    )
    out_specs = (P("dom", None, "grp"), P())
    return jax.shard_map(shards, mesh=mesh, in_specs=in_specs, out_specs=out_specs, check_vma=False)
```
